512 devices in a mesh: region: 128 (over z, y, core), chan: 4 (over x).
Axes of the slice: x: 4, y: 8, z: 8, core: 2. Of those that a mesh axis runs over, the one named last changes fastest.
Arguments:
- grid_state: bfloat16 [131072, 1024], P('region', 'chan'), may hold values from -6 to 6
- mesh_state: bfloat16 [32768, 1024], P('region', 'chan'), may hold values from -6 to 6
- enc_send: bfloat16 [1024, 1024], P(None, 'chan'), may hold values from -0.1875 to 0.1875
- enc_out: bfloat16 [1024, 1024], P(None, 'chan'), may hold values from -0.1875 to 0.1875
- proc_send: bfloat16 [1024, 1024], P(None, 'chan'), may hold values from -0.1875 to 0.1875
- proc_out: bfloat16 [1024, 1024], P(None, 'chan'), may hold values from -0.1875 to 0.1875
- dec_send: bfloat16 [1024, 1024], P(None, 'chan'), may hold values from -0.1875 to 0.1875
- dec_out: bfloat16 [1024, 1024], P(None, 'chan'), may hold values from -0.1875 to 0.1875
- g2m_index: int32 [16, 32768], P(None, 'region'), may hold values from 0 to 131071, as said below
- g2m_weight: float32 [16, 32768], P(None, 'region'), may hold values from 0.25 to 4
- g2m_count: int32 [32768], P('region'), may hold values from 1 to 16
- m2m_index: int32 [8, 32768], P(None, 'region'), may hold values from 0 to 32767, as said below
- m2m_weight: float32 [8, 32768], P(None, 'region'), may hold values from 0.25 to 4
- m2m_count: int32 [32768], P('region'), may hold values from 1 to 8
- m2g_index: int32 [4, 131072], P(None, 'region'), may hold values from 0 to 32767, as said below
- m2g_weight: float32 [4, 131072], P(None, 'region'), may hold values from 0.25 to 4
- m2g_count: int32 [131072], P('region'), may hold values from 1 to 4
Outputs:
- grid_next: bfloat16 [131072, 1024], P('region', 'chan')
- mesh_next: bfloat16 [32768, 1024], P('region', 'chan')
The draws below stay inside these ranges and needn't reach their ends.
Inputs may be any that keep to these rules, and one draw needn't show every extreme that they name: Column i of g2m_index belongs to mesh node i, of region i // 256; each entry names a grid node whose region (index // 1024) differs from it by at most 2. `m2m_index`: column i belongs to mesh node i, of region i // 256; each entry names a mesh node whose region (index // 256) differs from it by at most 2. `m2g_index`: column i belongs to grid node i, of region i // 1024; each entry names a mesh node whose region (index // 256) differs from it by at most 2.
All inputs are finite; a program needn't handle non-finite values.
Results may differ from the reference program's by a relative error of at most 0.017.
Values may be sent and summed in bfloat16 or wider, within the bound.
No kernel may reach another device: no remote copies, remote signals or barrier semaphores. Data moves between devices by JAX's collectives and lax.ppermute only.
A program may use at most 64 MiB of HBM per device.

```python
import math
import jax
import jax.numpy as jnp
from jax import lax

H = 1024
G_DEV = 1024
M_DEV = 256
K_E = 16
K_M = 8
K_D = 4
SPAN = 2
GRID = 131072
MESH = 32768
N_REGION = 128


def neighbours(key, fanin, recv_dev, send_dev, recv_total):
    regions = recv_total // recv_dev
    column = jnp.arange(recv_total, dtype=jnp.int32) // recv_dev
    key_offset, key_row = jax.random.split(key)
    offset = jax.random.randint(key_offset, (fanin, recv_total), -SPAN, SPAN + 1, dtype=jnp.int32)
    block = jnp.clip(column[None, :] + offset, 0, regions - 1)
    row_pick = jax.random.randint(key_row, (fanin, recv_total), 0, send_dev, dtype=jnp.int32)
    return (block * send_dev + row_pick).astype(jnp.int32)


def draw_g2m_index(key, part):
    key = jax.random.fold_in(key, 11)
    return neighbours(key, K_E, M_DEV, G_DEV, MESH)


def draw_m2m_index(key, part):
    key = jax.random.fold_in(key, 12)
    return neighbours(key, K_M, M_DEV, M_DEV, MESH)


def draw_m2g_index(key, part):
    key = jax.random.fold_in(key, 13)
    return neighbours(key, K_D, G_DEV, M_DEV, GRID)


def place_ends(result, key, least, top_value):
    longest = result.shape.index(max(result.shape))
    spots = []
    for shift in (0, 1):
        where = [jax.random.randint(jax.random.fold_in(key, axis), (), 0, length) for axis, length in enumerate(result.shape)]
        where[longest] = (where[longest] + shift) % result.shape[longest]
        spots.append(tuple(where))
    return result.at[spots[0]].set(least).at[spots[1]].set(top_value)


def block_levels(own_key, extent, cuts, smallest, largest):
    factor_of, own = 1.0, jax.random.fold_in(own_key, 6)
    for axis_at, parts in cuts:
        heights = jnp.exp(jax.random.uniform(jax.random.fold_in(own, axis_at), (parts,), jnp.float32, smallest / len(cuts), largest / len(cuts)))
        factor_of = factor_of * jnp.repeat(heights, extent[axis_at] // parts).reshape([-1 if axis == axis_at else 1 for axis in range(len(extent))])
    return factor_of


def gaussian(own_key, shape, spread, limit, cuts=(), held_as=jnp.bfloat16):
    loudness = block_levels(own_key, shape, cuts, -0.22, 0.18) if cuts else 1.0
    entries = jax.random.normal(own_key, shape, jnp.float32) * spread * loudness
    return jnp.minimum(jnp.maximum(entries, -limit), limit).astype(held_as)


def setup_inputs(seed: int = 0) -> dict:
    splits = jax.random.split(jax.random.key(seed), 18)
    return {
        "grid_state": gaussian(splits[0], (GRID, H), 1.0, 6.0, ((0, 128), (1, 4))),
        "mesh_state": gaussian(splits[1], (MESH, H), 1.0, 6.0, ((0, 128), (1, 4))),
        "enc_send": gaussian(splits[2], (H, H), H ** -0.5, 0.1875, ((1, 4),)),
        "enc_out": gaussian(splits[3], (H, H), H ** -0.5, 0.1875, ((1, 4),)),
        "proc_send": gaussian(splits[4], (H, H), H ** -0.5, 0.1875, ((1, 4),)),
        "proc_out": gaussian(splits[5], (H, H), H ** -0.5, 0.1875, ((1, 4),)),
        "dec_send": gaussian(splits[6], (H, H), H ** -0.5, 0.1875, ((1, 4),)),
        "dec_out": gaussian(splits[7], (H, H), H ** -0.5, 0.1875, ((1, 4),)),
        "g2m_index": draw_g2m_index(jax.random.fold_in(splits[17], 71), 0),
        "g2m_weight": jnp.clip(jnp.exp(math.log(4.0) - 2.7725887 * jax.random.uniform(splits[9], (K_E, MESH), jnp.float32) ** block_levels(splits[9], (K_E, MESH), ((1, 128),), -0.2, 0.2)), 0.25, 4.0),
        "g2m_count": place_ends(jax.random.randint(splits[10], (MESH,), 1, K_E + 1), jax.random.fold_in(splits[10], 1), 1, K_E).astype(jnp.int32),
        "m2m_index": draw_m2m_index(jax.random.fold_in(splits[17], 71), 0),
        "m2m_weight": jnp.clip(jnp.exp(math.log(4.0) - 2.7725887 * jax.random.uniform(splits[12], (K_M, MESH), jnp.float32) ** block_levels(splits[12], (K_M, MESH), ((1, 128),), -0.2, 0.2)), 0.25, 4.0),
        "m2m_count": place_ends(jax.random.randint(splits[13], (MESH,), 1, K_M + 1), jax.random.fold_in(splits[13], 1), 1, K_M).astype(jnp.int32),
        "m2g_index": draw_m2g_index(jax.random.fold_in(splits[17], 71), 0),
        "m2g_weight": jnp.clip(jnp.exp(math.log(4.0) - 2.7725887 * jax.random.uniform(splits[15], (K_D, GRID), jnp.float32) ** block_levels(splits[15], (K_D, GRID), ((1, 128),), -0.2, 0.2)), 0.25, 4.0),
        "m2g_count": place_ends(jax.random.randint(splits[16], (GRID,), 1, K_D + 1), jax.random.fold_in(splits[16], 1), 1, K_D).astype(jnp.int32),
    }


def messages(projected, receivers, index_block, edge_weight, counts):
    slots = index_block.shape[0]
    fetched = jnp.take(projected, index_block, axis=0).astype(jnp.float32)
    message = jax.nn.silu(fetched + receivers.astype(jnp.float32)[None]) * edge_weight[:, :, None]
    valid = jnp.arange(slots, dtype=jnp.int32)[:, None] < counts[None, :]
    summed = jnp.sum(jnp.where(valid[:, :, None], message, 0.0), axis=0)
    return (summed / counts.astype(jnp.float32)[:, None]).astype(jnp.bfloat16)


def layer(senders, receivers, w_send, w_out, index_block, edge_weight, counts):
    projected = jnp.dot(senders, w_send, preferred_element_type=jnp.float32).astype(jnp.bfloat16)
    slots = index_block.shape[0]
    per_region = receivers.shape[0] // N_REGION
    width = receivers.shape[1]
    recv_blocks = receivers.reshape(N_REGION, per_region, width)
    index_blocks = index_block.reshape(slots, N_REGION, per_region).transpose(1, 0, 2)
    weight_blocks = edge_weight.reshape(slots, N_REGION, per_region).transpose(1, 0, 2)
    count_blocks = counts.reshape(N_REGION, per_region)

    def one_block(items):
        return messages(projected, items[0], items[1], items[2], items[3])

    aggregate = lax.map(one_block, (recv_blocks, index_blocks, weight_blocks, count_blocks))
    aggregate = aggregate.reshape(receivers.shape[0], width)
    update = jnp.dot(aggregate, w_out, preferred_element_type=jnp.float32)
    return (receivers.astype(jnp.float32) + update).astype(jnp.bfloat16)


def reference(grid_state, mesh_state, enc_send, enc_out, proc_send, proc_out, dec_send, dec_out, g2m_index, g2m_weight, g2m_count, m2m_index, m2m_weight, m2m_count, m2g_index, m2g_weight, m2g_count):
    mesh_one = layer(grid_state, mesh_state, enc_send, enc_out, g2m_index, g2m_weight, g2m_count)
    mesh_next = layer(mesh_one, mesh_one, proc_send, proc_out, m2m_index, m2m_weight, m2m_count)
    grid_next = layer(mesh_next, grid_state, dec_send, dec_out, m2g_index, m2g_weight, m2g_count)
    return grid_next, mesh_next
```

```python
import functools

import jax
import jax.numpy as jnp
from jax import lax
from jax.experimental import pallas as pl
from jax.experimental.pallas import tpu as pltpu
from jax.sharding import PartitionSpec as P

LANES = 128
TILE = 8
VMEM = pl.BlockSpec(memory_space=pltpu.VMEM)
HBM = pl.BlockSpec(memory_space=pltpu.HBM)
SMEM = pl.BlockSpec(memory_space=pltpu.SMEM)


def exchange(shard, axis, partner):
    n = lax.axis_size(axis)
    return lax.ppermute(shard, axis, [(i, partner(i)) for i in range(n)])


def shift(shard, by):
    n = lax.axis_size("region")
    return lax.ppermute(shard, "region", [(i, i + by) for i in range(n) if 0 <= i + by < n])


def core_pair(shard):
    n = lax.axis_size("region")
    groups = [[i, i + 1] for i in range(0, n, 2)]
    return lax.all_gather(shard, "region", axis=0, tiled=True, axis_index_groups=groups)


def gather_chan(values):
    return lax.all_gather(values, "chan", axis=1, tiled=True)


def dot(a, b):
    return jnp.dot(a, b, preferred_element_type=jnp.float32)


def partial_kernel(me_ref, own, near_top, near_low, other_top, other_low, weight, total):
    me = me_ref[0]
    rows, width = own.shape
    half = rows // 2

    def block_of(source):
        return weight[pl.ds(pl.multiple_of(source * width, width), width), :]

    mine, near, other = block_of(me), block_of(me ^ 1), block_of(3 - me)
    for first, from_near, from_other in ((0, near_top, other_top), (half, near_low, other_low)):
        at = slice(first, first + half)
        total[at, :] = dot(own[at, :], mine) + dot(from_near[...], near) + dot(from_other[...], other)


def last_kernel(me_ref, total, far_top, far_low, weight, *refs):
    base, out = refs[:-1], refs[-1]
    rows, width = total.shape
    half = rows // 2
    block = weight[pl.ds(pl.multiple_of((me_ref[0] ^ 2) * width, width), width), :]
    for first, far in ((0, far_top), (half, far_low)):
        at = slice(first, first + half)
        value = total[at, :] + dot(far[...], block)
        for ref in base:
            value = value + ref[at, :].astype(jnp.float32)
        out[at, :] = value.astype(out.dtype)


def project_by_exchanges(values, weight, base=()):
    assert lax.axis_size("chan") == 4
    me = lax.axis_index("chan").astype(jnp.int32)[None]
    rows, width = values.shape
    half = rows // 2
    near = functools.partial(exchange, axis="chan", partner=lambda i: i ^ 1)
    other = functools.partial(exchange, axis="chan", partner=lambda i: 3 - i)
    top, low = values[:half], values[half:]
    other_top, near_low = other(top), near(low)
    other_low, near_top = other(low), near(top)
    far_top, far_low = near(other_top), other(near_low)
    params = pltpu.CompilerParams(vmem_limit_bytes=10 << 20)
    total = pl.pallas_call(
        partial_kernel,
        out_shape=jax.ShapeDtypeStruct((rows, width), jnp.float32),
        in_specs=[SMEM] + [VMEM] * 6,
        out_specs=VMEM,
        compiler_params=params,
        cost_estimate=pl.CostEstimate(flops=6 * rows * width * width, bytes_accessed=10 * rows * width, transcendentals=0),
        name="first_blocks",
    )(me, values, near_top, near_low, other_top, other_low, weight)
    return pl.pallas_call(
        last_kernel,
        out_shape=jax.ShapeDtypeStruct((rows, width), values.dtype),
        in_specs=[SMEM] + [VMEM] * (4 + len(base)),
        out_specs=VMEM,
        compiler_params=params,
        cost_estimate=pl.CostEstimate(flops=2 * rows * width * width, bytes_accessed=10 * rows * width, transcendentals=0),
        name="last_block",
    )(me, total, far_top, far_low, weight, *base)


def combine_kernel(rows_ref, first, second, mixed, base):
    rows, width = rows_ref[...], first.shape[1]
    for at, weight in ((slice(0, width), first), (slice(width, 2 * width), second)):
        value = dot(rows, weight[...])
        base[:, at] = value
        mixed[:, at] = value.astype(mixed.dtype)


def combine(gathered, first, second, block):
    rows, depth = gathered.shape
    width = first.shape[1]
    whole = pl.BlockSpec((depth, width), lambda i: (0, 0))
    return pl.pallas_call(
        combine_kernel,
        grid=(rows // block,),
        out_shape=(
            jax.ShapeDtypeStruct((rows, 2 * width), gathered.dtype),
            jax.ShapeDtypeStruct((block, 2 * width), jnp.float32),
        ),
        in_specs=[pl.BlockSpec((block, depth), lambda i: (i, 0)), whole, whole],
        out_specs=(
            pl.BlockSpec((block, 2 * width), lambda i: (i, 0)),
            pl.BlockSpec((block, 2 * width), lambda i: (0, 0)),
        ),
        compiler_params=pltpu.CompilerParams(vmem_limit_bytes=10 << 20),
        cost_estimate=pl.CostEstimate(flops=4 * rows * depth * width, bytes_accessed=2 * rows * depth, transcendentals=0),
        name="combine",
    )(gathered, first, second)


def halves_dot(core, full, mine, other, rows, columns):
    half = full.shape[1] // 2
    first = pl.multiple_of(core * half, half)
    second = pl.multiple_of((1 - core) * half, half)
    return dot(full[:, pl.ds(first, half)], mine[rows, columns]) + dot(full[:, pl.ds(second, half)], other[rows, columns])


def mesh_one_kernel(core_ref, full, mesh, w_out, mine, other, base, mesh_one, projected, later):
    core, width = core_ref[0], mesh.shape[1]
    half = full.shape[1] // 2
    rows, one, two = slice(0, half), slice(0, width), slice(width, 2 * width)
    mesh_one[...] = (mesh[...].astype(jnp.float32) + dot(full[...], w_out[...])).astype(mesh_one.dtype)
    projected[...] = (base[:, one] + halves_dot(core, full, mine, other, rows, one)).astype(projected.dtype)
    later[...] = base[:, two] + halves_dot(core, full, mine, other, rows, two)


def mesh_next_kernel(core_ref, full, mesh_one, w_out, mine, other, later, mesh_next, projected):
    core, width = core_ref[0], mesh_one.shape[1]
    half = full.shape[1] // 2
    rows, two = slice(half, 2 * half), slice(width, 2 * width)
    mesh_next[...] = (mesh_one[...].astype(jnp.float32) + dot(full[...], w_out[...])).astype(mesh_next.dtype)
    projected[...] = (later[...] + halves_dot(core, full, mine, other, rows, two)).astype(projected.dtype)


def mesh_step(kernel, like, kinds, core, *operands):
    return pl.pallas_call(
        kernel,
        out_shape=[jax.ShapeDtypeStruct(like.shape, kind) for kind in kinds],
        in_specs=[SMEM] + [VMEM] * len(operands),
        out_specs=[VMEM] * len(kinds),
        compiler_params=pltpu.CompilerParams(vmem_limit_bytes=10 << 20),
        cost_estimate=pl.CostEstimate(flops=len(kinds) << 27, bytes_accessed=1 << 22, transcendentals=0),
        name="mesh_step",
    )(core, *operands)


def window_of_exchanges(projected):
    below = shift(projected, 2)
    above = shift(projected, -2)
    other = exchange(projected, "region", lambda i: i ^ 1)
    first = lax.axis_index("region") % 2 == 0
    third = exchange(jnp.where(first, above, below), "region", lambda i: i ^ 1)
    return [projected, below, above, other, third]


def window_of_pairs(projected):
    below = shift(projected, 2)
    above = shift(projected, -2)
    own = core_pair(projected)
    first = lax.axis_index("region") % 2 == 0
    outer = core_pair(jnp.where(first, above, below))
    last = jnp.where(first, below, above)
    return [outer, own, last]


def edges_kernel(n_grid, n_mesh, me_ref, *refs):
    sources, (o1, s1, o2, s2, o3, s3) = refs[:9], refs[9:15]
    i1, w1, c1, i2, w2, c2, i3, w3, c3 = held = refs[15:24]
    copies = [pltpu.make_async_copy(src, dst, refs[24].at[k]) for k, (src, dst) in enumerate(zip(sources, held))]
    for copy in copies:
        copy.start()
    for copy in copies:
        copy.wait()
    me = me_ref[0]
    core = me & 1

    def of_exchanges(apart):
        towards = 1 - 2 * core
        return jnp.where(apart == 0, 0, jnp.where(apart == -2, 1, jnp.where(apart == 2, 2, jnp.where(apart == towards, 3, 4))))

    def of_pairs(apart):
        apart = apart + core
        return jnp.where(apart == 2, 0, jnp.where(apart == -1, 1, jnp.where(apart == 0, 2, jnp.where(apart == 1, 3, 4))))

    def place(index, rows, piece):
        shift_by = rows.bit_length() - 1
        return (piece((index >> shift_by) - me) << shift_by) + (index & (rows - 1))

    def scaled(w, c):
        live = lax.broadcasted_iota(jnp.int32, w.shape, 0) < c[...]
        return jnp.where(live, w[...], 0.0) / c[...].astype(jnp.float32)

    def upright(v):
        if v.shape[0] < TILE:
            v = jnp.concatenate([v, jnp.zeros((TILE - v.shape[0], v.shape[1]), v.dtype)], axis=0)
        return v.T

    o1[...] = 2 * place(i1[...], n_grid, of_exchanges)
    tall = upright(scaled(w1, c1))
    for s in range(2):
        s1[pl.ds(s, tall.shape[0], 2), :] = tall
    o2[...] = upright(place(i2[...], n_mesh, of_pairs))
    s2[...] = upright(scaled(w2, c2))
    o3[...] = upright(place(i3[...], n_mesh, of_pairs))
    s3[...] = upright(scaled(w3, c3))


def edges(n_grid, n_mesh, g2m, m2m, m2g):
    me = lax.axis_index("region").astype(jnp.int32)[None]
    ops, outs = [me], []
    for at, (index, weight, count) in enumerate((g2m, m2m, m2g)):
        slots, rows = index.shape
        ops += [index, weight, count[None, :]]
        high = max(slots, TILE)
        outs += [
            jax.ShapeDtypeStruct((slots, rows) if at == 0 else (rows, high), jnp.int32),
            jax.ShapeDtypeStruct((2 * rows if at == 0 else rows, high), jnp.float32),
        ]
    return pl.pallas_call(
        functools.partial(edges_kernel, n_grid, n_mesh),
        out_shape=outs,
        in_specs=[SMEM] + [HBM] * 9,
        out_specs=[VMEM] * 6,
        scratch_shapes=[pltpu.VMEM(op.shape, op.dtype) for op in ops[1:]] + [pltpu.SemaphoreType.DMA((9,))],
        compiler_params=pltpu.CompilerParams(vmem_limit_bytes=60 << 20),
        cost_estimate=pl.CostEstimate(flops=1 << 20, bytes_accessed=1 << 20, transcendentals=0),
        name="edges",
    )(*ops)


def by_rows_kernel(slots, rows, group, sizes, index_ref, weight_ref, receiver_ref, *refs):
    parts, out_ref = refs[: len(sizes)], refs[len(sizes)]
    window, receiver, fetched, total = refs[len(sizes) + 1 :]
    first = 0
    for part, size in zip(parts, sizes):
        half = part[...].astype(jnp.float32) * 0.5
        for s in range(2):
            window[pl.ds(2 * first + s, size, 2), :] = half[:, s * LANES : (s + 1) * LANES]
        first += size
    half = receiver_ref[...].astype(jnp.float32) * 0.5
    for s in range(2):
        receiver[pl.ds(s, rows, 2), :] = half[:, s * LANES : (s + 1) * LANES]

    def fetch(start, side):
        for u in range(group):
            for k in range(slots):
                at = ((u // 4) * slots + k) * TILE + (u % 4) * 2
                fetched[side, at : at + 2, :] = window[pl.ds(index_ref[k, start + u], 2), :]

    def add_up(start, side):
        for t in range(group // 4):
            row = pl.multiple_of(2 * start + TILE * t, TILE)
            mine = receiver[pl.ds(row, TILE), :]
            weight = weight_ref[pl.ds(row, TILE), :]
            acc = jnp.zeros((TILE, LANES), jnp.float32)
            for k in range(slots):
                at = (t * slots + k) * TILE
                h = fetched[side, at : at + TILE, :] + mine
                acc = acc + (h + h * jnp.tanh(h)) * weight[:, k : k + 1]
            total[pl.ds(row, TILE), :] = acc

    fetch(0, 0)

    def two_groups(j, carry):
        start = j * 2 * group
        fetch(start + group, 1)
        add_up(start, 0)
        fetch(jnp.minimum(start + 2 * group, rows - group), 0)
        add_up(start + group, 1)
        return carry

    lax.fori_loop(0, rows // (2 * group), two_groups, 0)
    for s in range(2):
        out_ref[:, s * LANES : (s + 1) * LANES] = total[pl.ds(s, rows, 2), :].astype(out_ref.dtype)


def aggregate_by_rows(index, weights, receivers, parts, group=8):
    slots, rows = index.shape
    width = receivers.shape[1]
    sizes = tuple(part.shape[0] for part in parts)
    return pl.pallas_call(
        functools.partial(by_rows_kernel, slots, rows, group, sizes),
        out_shape=jax.ShapeDtypeStruct((rows, width), receivers.dtype),
        in_specs=[SMEM] + [VMEM] * (2 + len(parts)),
        out_specs=VMEM,
        scratch_shapes=[
            pltpu.VMEM((2 * sum(sizes), LANES), jnp.float32),
            pltpu.VMEM((2 * rows, LANES), jnp.float32),
            pltpu.VMEM((2, group // 4 * slots * TILE, LANES), jnp.float32),
            pltpu.VMEM((2 * rows, LANES), jnp.float32),
        ],
        compiler_params=pltpu.CompilerParams(vmem_limit_bytes=14 << 20),
        cost_estimate=pl.CostEstimate(
            flops=6 * slots * rows * width,
            bytes_accessed=2 * width * (sum(sizes) + 2 * rows),
            transcendentals=slots * rows * width,
        ),
        name="aggregate_by_rows",
    )(index, weights, receivers, *parts)


def by_matmul_kernel(slots, rows, block, sizes, index_ref, weight_ref, receiver_ref, *refs):
    parts, out_ref, window = refs[: len(sizes)], refs[len(sizes)], refs[len(sizes) + 1]
    first = 0
    for part, size in zip(parts, sizes):
        window[first : first + size, :] = part[...]
        first += size
    columns = lax.broadcasted_iota(jnp.int32, (block, first), 1).astype(jnp.int16)
    one, zero = jnp.bfloat16(1), jnp.bfloat16(0)

    def one_block(b, carry):
        at = pl.ds(pl.multiple_of(b * block, block), block)
        mine = receiver_ref[at, :].astype(jnp.float32)
        index, weight = index_ref[at, :], weight_ref[at, :]
        acc = jnp.zeros(mine.shape, jnp.float32)
        for k in range(slots):
            wanted = jnp.broadcast_to(index[:, k : k + 1], (block, LANES)).astype(jnp.int16)
            pick = [jnp.where(columns[:, j : j + LANES] == wanted, one, zero) for j in range(0, first, LANES)]
            fetched = dot(jnp.concatenate(pick, axis=1), window[...])
            h = (fetched + mine) * 0.5
            acc = acc + (h + h * jnp.tanh(h)) * weight[:, k : k + 1]
        out_ref[at, :] = acc.astype(out_ref.dtype)
        return carry

    lax.fori_loop(0, rows // block, one_block, 0)


def aggregate_by_matmul(slots, index, weights, receivers, parts, block=256):
    rows, width = receivers.shape
    sizes = tuple(part.shape[0] for part in parts)
    return pl.pallas_call(
        functools.partial(by_matmul_kernel, slots, rows, block, sizes),
        out_shape=jax.ShapeDtypeStruct((rows, width), receivers.dtype),
        in_specs=[VMEM] * (3 + len(parts)),
        out_specs=VMEM,
        scratch_shapes=[pltpu.VMEM((sum(sizes), width), jnp.bfloat16)],
        compiler_params=pltpu.CompilerParams(vmem_limit_bytes=14 << 20),
        cost_estimate=pl.CostEstimate(
            flops=2 * slots * rows * sum(sizes) * width,
            bytes_accessed=2 * width * (sum(sizes) + 2 * rows),
            transcendentals=slots * rows * width,
        ),
        name="aggregate_by_matmul",
    )(index, weights, receivers, *parts)


def shards(
    grid_state,
    mesh_state,
    enc_send,
    enc_out,
    proc_send,
    proc_out,
    dec_send,
    dec_out,
    g2m_index,
    g2m_weight,
    g2m_count,
    m2m_index,
    m2m_weight,
    m2m_count,
    m2g_index,
    m2g_weight,
    m2g_count,
):
    n_grid, n_mesh = grid_state.shape[0], mesh_state.shape[0]
    bf16, f32 = jnp.bfloat16, jnp.float32
    k_m, k_d = m2m_index.shape[0], m2g_index.shape[0]
    prepared = edges(
        n_grid,
        n_mesh,
        (g2m_index, g2m_weight, g2m_count),
        (m2m_index, m2m_weight, m2m_count),
        (m2g_index, m2g_weight, m2g_count),
    )

    grid_state, prepared = lax.optimization_barrier((grid_state, prepared))
    g2m, g2m_w, m2m, m2m_w, m2g, m2g_w = prepared

    core = lax.axis_index("region").astype(jnp.int32) % 2
    half = enc_out.shape[0] // 2
    own_rows = [lax.dynamic_slice_in_dim(w, core * half, half, axis=0) for w in (enc_out, proc_out)]
    gathered = gather_chan(jnp.concatenate(own_rows + [mesh_state], axis=0))

    projected = project_by_exchanges(grid_state, enc_send)
    agg = aggregate_by_rows(g2m, g2m_w, mesh_state, window_of_exchanges(projected))

    agg, gathered = lax.optimization_barrier((agg, gathered))
    mine, base = combine(gathered, proc_send, dec_send, n_mesh)
    other = exchange(mine[: 2 * half], "region", lambda i: i ^ 1)
    agg, base = lax.optimization_barrier((agg, base))
    mesh_one, projected, later = mesh_step(
        mesh_one_kernel, mesh_state, (bf16, bf16, f32), core[None], gather_chan(agg), mesh_state, enc_out, mine, other, base
    )
    agg = aggregate_by_matmul(k_m, m2m, m2m_w, mesh_one, window_of_pairs(projected))
    mesh_next, projected = mesh_step(
        mesh_next_kernel, mesh_state, (bf16, bf16), core[None], gather_chan(agg), mesh_one, proc_out, mine, other, later
    )
    agg = aggregate_by_matmul(k_d, m2g, m2g_w, grid_state, window_of_pairs(projected))
    grid_next = project_by_exchanges(agg, dec_out, base=(grid_state,))
    return grid_next, mesh_next


def solution(mesh):
    by_both, by_chan = P("region", "chan"), P(None, "chan")
    edge = (P(None, "region"), P(None, "region"), P("region"))
    return jax.shard_map(
        shards,
        mesh=mesh,
        in_specs=(by_both,) * 2 + (by_chan,) * 6 + edge * 3,
        out_specs=(by_both, by_both),
        check_vma=False,
    )
```

```python
import functools

import jax
import jax.numpy as jnp
from jax import lax
from jax.experimental import pallas as pl
from jax.experimental.pallas import tpu as pltpu
from jax.sharding import PartitionSpec as P

LANES = 128
TILE = 8
VMEM = pl.BlockSpec(memory_space=pltpu.VMEM)
HBM = pl.BlockSpec(memory_space=pltpu.HBM)
SMEM = pl.BlockSpec(memory_space=pltpu.SMEM)


def exchange(shard, axis, partner):
    n = lax.axis_size(axis)
    return lax.ppermute(shard, axis, [(i, partner(i)) for i in range(n)])


def shift(shard, by):
    n = lax.axis_size("region")
    return lax.ppermute(shard, "region", [(i, i + by) for i in range(n) if 0 <= i + by < n])


def core_pair(shard):
    n = lax.axis_size("region")
    groups = [[i, i + 1] for i in range(0, n, 2)]
    return lax.all_gather(shard, "region", axis=0, tiled=True, axis_index_groups=groups)


def gather_chan(values):
    return lax.all_gather(values, "chan", axis=1, tiled=True)


def dot(a, b):
    return jnp.dot(a, b, preferred_element_type=jnp.float32)


def partial_kernel(me_ref, own, near_top, near_low, other_top, other_low, weight, total):
    me = me_ref[0]
    rows, width = own.shape
    half = rows // 2

    def block_of(source):
        return weight[pl.ds(pl.multiple_of(source * width, width), width), :]

    mine, near, other = block_of(me), block_of(me ^ 1), block_of(3 - me)
    for first, from_near, from_other in ((0, near_top, other_top), (half, near_low, other_low)):
        at = slice(first, first + half)
        total[at, :] = dot(own[at, :], mine) + dot(from_near[...], near) + dot(from_other[...], other)


def last_kernel(me_ref, total, far_top, far_low, weight, *refs):
    base, out = refs[:-1], refs[-1]
    rows, width = total.shape
    half = rows // 2
    block = weight[pl.ds(pl.multiple_of((me_ref[0] ^ 2) * width, width), width), :]
    for first, far in ((0, far_top), (half, far_low)):
        at = slice(first, first + half)
        value = total[at, :] + dot(far[...], block)
        for ref in base:
            value = value + ref[at, :].astype(jnp.float32)
        out[at, :] = value.astype(out.dtype)


def project_by_exchanges(values, weight, base=(), later=None):
    assert lax.axis_size("chan") == 4
    me = lax.axis_index("chan").astype(jnp.int32)[None]
    rows, width = values.shape
    half = rows // 2
    near = functools.partial(exchange, axis="chan", partner=lambda i: i ^ 1)
    other = functools.partial(exchange, axis="chan", partner=lambda i: 3 - i)
    top, low = values[:half], values[half:]
    other_top, near_low = other(top), near(low)
    other_low, near_top = other(low), near(top)
    far_top, far_low = near(other_top), other(near_low)
    params = pltpu.CompilerParams(vmem_limit_bytes=10 << 20)
    total = pl.pallas_call(
        partial_kernel,
        out_shape=jax.ShapeDtypeStruct((rows, width), jnp.float32),
        in_specs=[SMEM] + [VMEM] * 6,
        out_specs=VMEM,
        compiler_params=params,
        cost_estimate=pl.CostEstimate(flops=6 * rows * width * width, bytes_accessed=10 * rows * width, transcendentals=0),
        name="first_blocks",
    )(me, values, near_top, near_low, other_top, other_low, weight)
    if later is not None:
        total, later = lax.optimization_barrier((total, later))
        later = exchange(later, "chan", lambda i: i ^ 2)
    out = pl.pallas_call(
        last_kernel,
        out_shape=jax.ShapeDtypeStruct((rows, width), values.dtype),
        in_specs=[SMEM] + [VMEM] * (4 + len(base)),
        out_specs=VMEM,
        compiler_params=params,
        cost_estimate=pl.CostEstimate(flops=2 * rows * width * width, bytes_accessed=10 * rows * width, transcendentals=0),
        name="last_block",
    )(me, total, far_top, far_low, weight, *base)
    return out, later


def combine_kernel(me_ref, own, near, other, far, first, second, mixed, base):
    me, width = me_ref[0], own.shape[1]
    rows, last = own.shape[0], base.shape[0]

    def one_block(start, size, targets):
        at = pl.ds(start, size)
        for column, weight in ((slice(0, width), first), (slice(width, 2 * width), second)):
            value = jnp.zeros((size, width), jnp.float32)
            for source, block in ((me, own), (me ^ 1, near), (3 - me, other), (me ^ 2, far)):
                value += dot(block[at, :], weight[pl.ds(pl.multiple_of(source * width, width), width), :])
            for target, to in targets:
                target[to, column] = value.astype(target.dtype)

    for start in range(0, rows - last, last):
        one_block(start, last, [(mixed, pl.ds(start, last))])
    one_block(rows - last, last, [(base, pl.ds(0, last))])


def combine(blocks, first, second, last):
    rows, width = blocks[0].shape
    return pl.pallas_call(
        combine_kernel,
        out_shape=(
            jax.ShapeDtypeStruct((rows - last, 2 * width), blocks[0].dtype),
            jax.ShapeDtypeStruct((last, 2 * width), jnp.float32),
        ),
        in_specs=[SMEM] + [VMEM] * 6,
        out_specs=(VMEM, VMEM),
        compiler_params=pltpu.CompilerParams(vmem_limit_bytes=10 << 20),
        cost_estimate=pl.CostEstimate(flops=16 * rows * width * width, bytes_accessed=16 * rows * width, transcendentals=0),
        name="combine",
    )(lax.axis_index("chan").astype(jnp.int32)[None], *blocks, first, second)


def halves_dot(core, full, mine, other, rows, columns):
    half = full.shape[1] // 2
    first = pl.multiple_of(core * half, half)
    second = pl.multiple_of((1 - core) * half, half)
    return dot(full[:, pl.ds(first, half)], mine[rows, columns]) + dot(full[:, pl.ds(second, half)], other[rows, columns])


def mesh_one_kernel(core_ref, full, mesh, w_out, mine, other, base, mesh_one, projected, later):
    core, width = core_ref[0], mesh.shape[1]
    half = full.shape[1] // 2
    rows, one, two = slice(0, half), slice(0, width), slice(width, 2 * width)
    mesh_one[...] = (mesh[...].astype(jnp.float32) + dot(full[...], w_out[...])).astype(mesh_one.dtype)
    projected[...] = (base[:, one] + halves_dot(core, full, mine, other, rows, one)).astype(projected.dtype)
    later[...] = base[:, two] + halves_dot(core, full, mine, other, rows, two)


def mesh_next_kernel(core_ref, full, mesh_one, w_out, mine, other, later, mesh_next, projected):
    core, width = core_ref[0], mesh_one.shape[1]
    half = full.shape[1] // 2
    rows, two = slice(half, 2 * half), slice(width, 2 * width)
    mesh_next[...] = (mesh_one[...].astype(jnp.float32) + dot(full[...], w_out[...])).astype(mesh_next.dtype)
    projected[...] = (later[...] + halves_dot(core, full, mine, other, rows, two)).astype(projected.dtype)


def mesh_step(kernel, like, kinds, core, *operands):
    return pl.pallas_call(
        kernel,
        out_shape=[jax.ShapeDtypeStruct(like.shape, kind) for kind in kinds],
        in_specs=[SMEM] + [VMEM] * len(operands),
        out_specs=[VMEM] * len(kinds),
        compiler_params=pltpu.CompilerParams(vmem_limit_bytes=10 << 20),
        cost_estimate=pl.CostEstimate(flops=len(kinds) << 27, bytes_accessed=1 << 22, transcendentals=0),
        name="mesh_step",
    )(core, *operands)


def window_of_exchanges(projected, later):
    below = shift(projected, 2)
    above = shift(projected, -2)
    other = exchange(projected, "region", lambda i: i ^ 1)
    other, later = lax.optimization_barrier((other, later))
    sent = [exchange(later, "chan", lambda i: i ^ 1), exchange(later, "chan", lambda i: 3 - i)]
    first = lax.axis_index("region") % 2 == 0
    third = exchange(jnp.where(first, above, below), "region", lambda i: i ^ 1)
    return [projected, below, above, other, third], sent


def window_of_pairs(projected):
    below = shift(projected, 2)
    above = shift(projected, -2)
    own = core_pair(projected)
    first = lax.axis_index("region") % 2 == 0
    outer = core_pair(jnp.where(first, above, below))
    last = jnp.where(first, below, above)
    return [outer, own, last]


def edges_kernel(n_grid, n_mesh, me_ref, *refs):
    sources, (first, second, mesh), (o1, s1, o2, s2, o3, s3, packed) = refs[:9], refs[9:12], refs[12:19]
    i1, w1, c1, i2, w2, c2, i3, w3, c3 = held = refs[19:28]
    semaphores = refs[28]
    me = me_ref[0]
    half = first.shape[0] // 2
    mine = pl.ds(pl.multiple_of((me & 1) * half, half), half)
    moves = list(zip(sources, held)) + [
        (first.at[mine, :], packed.at[pl.ds(0, half), :]),
        (second.at[mine, :], packed.at[pl.ds(half, half), :]),
        (mesh, packed.at[pl.ds(2 * half, mesh.shape[0]), :]),
    ]
    copies = [pltpu.make_async_copy(src, dst, semaphores.at[k]) for k, (src, dst) in enumerate(moves)]
    for copy in copies:
        copy.start()
    for copy in copies:
        copy.wait()
    core = me & 1

    def of_exchanges(apart):
        towards = 1 - 2 * core
        return jnp.where(apart == 0, 0, jnp.where(apart == -2, 1, jnp.where(apart == 2, 2, jnp.where(apart == towards, 3, 4))))

    def of_pairs(apart):
        apart = apart + core
        return jnp.where(apart == 2, 0, jnp.where(apart == -1, 1, jnp.where(apart == 0, 2, jnp.where(apart == 1, 3, 4))))

    def place(index, rows, piece):
        shift_by = rows.bit_length() - 1
        return (piece((index >> shift_by) - me) << shift_by) + (index & (rows - 1))

    def scaled(w, c):
        live = lax.broadcasted_iota(jnp.int32, w.shape, 0) < c[...]
        return jnp.where(live, w[...], 0.0) / c[...].astype(jnp.float32)

    def upright(v):
        if v.shape[0] < TILE:
            v = jnp.concatenate([v, jnp.zeros((TILE - v.shape[0], v.shape[1]), v.dtype)], axis=0)
        return v.T

    o1[...] = 2 * place(i1[...], n_grid, of_exchanges)
    tall = upright(scaled(w1, c1))
    for s in range(2):
        s1[pl.ds(s, tall.shape[0], 2), :] = tall
    o2[...] = upright(place(i2[...], n_mesh, of_pairs))
    s2[...] = upright(scaled(w2, c2))
    o3[...] = upright(place(i3[...], n_mesh, of_pairs))
    s3[...] = upright(scaled(w3, c3))


def edges(n_grid, n_mesh, g2m, m2m, m2g, first, second, mesh):
    me = lax.axis_index("region").astype(jnp.int32)[None]
    ops, outs = [me], []
    for at, (index, weight, count) in enumerate((g2m, m2m, m2g)):
        slots, rows = index.shape
        ops += [index, weight, count[None, :]]
        high = max(slots, TILE)
        outs += [
            jax.ShapeDtypeStruct((slots, rows) if at == 0 else (rows, high), jnp.int32),
            jax.ShapeDtypeStruct((2 * rows if at == 0 else rows, high), jnp.float32),
        ]
    packed = (first.shape[0] + mesh.shape[0], mesh.shape[1])
    outs.append(jax.ShapeDtypeStruct(packed, mesh.dtype))
    return pl.pallas_call(
        functools.partial(edges_kernel, n_grid, n_mesh),
        out_shape=outs,
        in_specs=[SMEM] + [HBM] * 12,
        out_specs=[VMEM] * 7,
        scratch_shapes=[pltpu.VMEM(op.shape, op.dtype) for op in ops[1:]] + [pltpu.SemaphoreType.DMA((12,))],
        compiler_params=pltpu.CompilerParams(vmem_limit_bytes=60 << 20),
        cost_estimate=pl.CostEstimate(flops=1 << 20, bytes_accessed=1 << 20, transcendentals=0),
        name="edges",
    )(*ops, first, second, mesh)


def by_rows_kernel(slots, rows, group, sizes, index_ref, weight_ref, receiver_ref, *refs):
    parts, out_ref = refs[: len(sizes)], refs[len(sizes)]
    window, receiver, fetched, total = refs[len(sizes) + 1 :]
    first = 0
    for part, size in zip(parts, sizes):
        half = part[...].astype(jnp.float32) * 0.5
        for s in range(2):
            window[pl.ds(2 * first + s, size, 2), :] = half[:, s * LANES : (s + 1) * LANES]
        first += size
    half = receiver_ref[...].astype(jnp.float32) * 0.5
    for s in range(2):
        receiver[pl.ds(s, rows, 2), :] = half[:, s * LANES : (s + 1) * LANES]

    def fetch(start, side):
        for u in range(group):
            for k in range(slots):
                at = ((u // 4) * slots + k) * TILE + (u % 4) * 2
                fetched[side, at : at + 2, :] = window[pl.ds(index_ref[k, start + u], 2), :]

    def add_up(start, side):
        for t in range(group // 4):
            row = pl.multiple_of(2 * start + TILE * t, TILE)
            mine = receiver[pl.ds(row, TILE), :]
            weight = weight_ref[pl.ds(row, TILE), :]
            acc = jnp.zeros((TILE, LANES), jnp.float32)
            for k in range(slots):
                at = (t * slots + k) * TILE
                h = fetched[side, at : at + TILE, :] + mine
                acc = acc + (h + h * jnp.tanh(h)) * weight[:, k : k + 1]
            total[pl.ds(row, TILE), :] = acc

    fetch(0, 0)

    def two_groups(j, carry):
        start = j * 2 * group
        fetch(start + group, 1)
        add_up(start, 0)
        fetch(jnp.minimum(start + 2 * group, rows - group), 0)
        add_up(start + group, 1)
        return carry

    lax.fori_loop(0, rows // (2 * group), two_groups, 0)
    for s in range(2):
        out_ref[:, s * LANES : (s + 1) * LANES] = total[pl.ds(s, rows, 2), :].astype(out_ref.dtype)


def aggregate_by_rows(index, weights, receivers, parts, group=8):
    slots, rows = index.shape
    width = receivers.shape[1]
    sizes = tuple(part.shape[0] for part in parts)
    return pl.pallas_call(
        functools.partial(by_rows_kernel, slots, rows, group, sizes),
        out_shape=jax.ShapeDtypeStruct((rows, width), receivers.dtype),
        in_specs=[SMEM] + [VMEM] * (2 + len(parts)),
        out_specs=VMEM,
        scratch_shapes=[
            pltpu.VMEM((2 * sum(sizes), LANES), jnp.float32),
            pltpu.VMEM((2 * rows, LANES), jnp.float32),
            pltpu.VMEM((2, group // 4 * slots * TILE, LANES), jnp.float32),
            pltpu.VMEM((2 * rows, LANES), jnp.float32),
        ],
        compiler_params=pltpu.CompilerParams(vmem_limit_bytes=14 << 20),
        cost_estimate=pl.CostEstimate(
            flops=6 * slots * rows * width,
            bytes_accessed=2 * width * (sum(sizes) + 2 * rows),
            transcendentals=slots * rows * width,
        ),
        name="aggregate_by_rows",
    )(index, weights, receivers, *parts)


def by_matmul_kernel(slots, rows, block, sizes, index_ref, weight_ref, receiver_ref, *refs):
    parts, out_ref, window = refs[: len(sizes)], refs[len(sizes)], refs[len(sizes) + 1]
    first = 0
    for part, size in zip(parts, sizes):
        window[first : first + size, :] = part[...]
        first += size
    columns = lax.broadcasted_iota(jnp.int32, (block, first), 1).astype(jnp.int16)
    one, zero = jnp.bfloat16(1), jnp.bfloat16(0)

    def one_block(b, carry):
        at = pl.ds(pl.multiple_of(b * block, block), block)
        mine = receiver_ref[at, :].astype(jnp.float32)
        index, weight = index_ref[at, :], weight_ref[at, :]
        acc = jnp.zeros(mine.shape, jnp.float32)
        for k in range(slots):
            wanted = jnp.broadcast_to(index[:, k : k + 1], (block, LANES)).astype(jnp.int16)
            pick = [jnp.where(columns[:, j : j + LANES] == wanted, one, zero) for j in range(0, first, LANES)]
            fetched = dot(jnp.concatenate(pick, axis=1), window[...])
            h = (fetched + mine) * 0.5
            acc = acc + (h + h * jnp.tanh(h)) * weight[:, k : k + 1]
        out_ref[at, :] = acc.astype(out_ref.dtype)
        return carry

    lax.fori_loop(0, rows // block, one_block, 0)


def aggregate_by_matmul(slots, index, weights, receivers, parts, block=256):
    rows, width = receivers.shape
    sizes = tuple(part.shape[0] for part in parts)
    return pl.pallas_call(
        functools.partial(by_matmul_kernel, slots, rows, block, sizes),
        out_shape=jax.ShapeDtypeStruct((rows, width), receivers.dtype),
        in_specs=[VMEM] * (3 + len(parts)),
        out_specs=VMEM,
        scratch_shapes=[pltpu.VMEM((sum(sizes), width), jnp.bfloat16)],
        compiler_params=pltpu.CompilerParams(vmem_limit_bytes=14 << 20),
        cost_estimate=pl.CostEstimate(
            flops=2 * slots * rows * sum(sizes) * width,
            bytes_accessed=2 * width * (sum(sizes) + 2 * rows),
            transcendentals=slots * rows * width,
        ),
        name="aggregate_by_matmul",
    )(index, weights, receivers, *parts)


def shards(
    grid_state,
    mesh_state,
    enc_send,
    enc_out,
    proc_send,
    proc_out,
    dec_send,
    dec_out,
    g2m_index,
    g2m_weight,
    g2m_count,
    m2m_index,
    m2m_weight,
    m2m_count,
    m2g_index,
    m2g_weight,
    m2g_count,
):
    n_grid, n_mesh = grid_state.shape[0], mesh_state.shape[0]
    bf16, f32 = jnp.bfloat16, jnp.float32
    k_m, k_d = m2m_index.shape[0], m2g_index.shape[0]
    core = lax.axis_index("region").astype(jnp.int32) % 2
    prepared = edges(
        n_grid,
        n_mesh,
        (g2m_index, g2m_weight, g2m_count),
        (m2m_index, m2m_weight, m2m_count),
        (m2g_index, m2g_weight, m2g_count),
        enc_out,
        proc_out,
        mesh_state,
    )
    grid_state, prepared = lax.optimization_barrier((grid_state, prepared))
    g2m, g2m_w, m2m, m2m_w, m2g, m2g_w, packed = prepared

    projected, far = project_by_exchanges(grid_state, enc_send, later=packed)
    window, nearer = window_of_exchanges(projected, packed)
    agg = aggregate_by_rows(g2m, g2m_w, mesh_state, window)

    agg, packed, nearer, far = lax.optimization_barrier((agg, packed, nearer, far))
    mine, base = combine([packed, *nearer, far], proc_send, dec_send, n_mesh)
    other = exchange(mine, "region", lambda i: i ^ 1)
    agg, base = lax.optimization_barrier((agg, base))
    mesh_one, projected, later = mesh_step(
        mesh_one_kernel, mesh_state, (bf16, bf16, f32), core[None], gather_chan(agg), mesh_state, enc_out, mine, other, base
    )
    agg = aggregate_by_matmul(k_m, m2m, m2m_w, mesh_one, window_of_pairs(projected))
    mesh_next, projected = mesh_step(
        mesh_next_kernel, mesh_state, (bf16, bf16), core[None], gather_chan(agg), mesh_one, proc_out, mine, other, later
    )
    agg = aggregate_by_matmul(k_d, m2g, m2g_w, grid_state, window_of_pairs(projected))
    grid_next, _ = project_by_exchanges(agg, dec_out, base=(grid_state,))
    return grid_next, mesh_next


def solution(mesh):
    by_both, by_chan = P("region", "chan"), P(None, "chan")
    edge = (P(None, "region"), P(None, "region"), P("region"))
    return jax.shard_map(
        shards,
        mesh=mesh,
        in_specs=(by_both,) * 2 + (by_chan,) * 6 + edge * 3,
        out_specs=(by_both, by_both),
        check_vma=False,
    )
```

```python
import functools

import jax
import jax.numpy as jnp
from jax import lax
from jax.experimental import pallas as pl
from jax.experimental.pallas import tpu as pltpu
from jax.sharding import PartitionSpec as P

LANES = 128
TILE = 8
VMEM = pl.BlockSpec(memory_space=pltpu.VMEM)
HBM = pl.BlockSpec(memory_space=pltpu.HBM)
SMEM = pl.BlockSpec(memory_space=pltpu.SMEM)


def exchange(shard, axis, partner):
    n = lax.axis_size(axis)
    return lax.ppermute(shard, axis, [(i, partner(i)) for i in range(n)])


def shift(shard, by):
    n = lax.axis_size("region")
    return lax.ppermute(shard, "region", [(i, i + by) for i in range(n) if 0 <= i + by < n])


def core_pair(shard):
    n = lax.axis_size("region")
    groups = [[i, i + 1] for i in range(0, n, 2)]
    return lax.all_gather(shard, "region", axis=0, tiled=True, axis_index_groups=groups)


def gather_chan(copies):
    return lax.all_to_all(copies, "chan", split_axis=0, concat_axis=0, tiled=True)


def dot(a, b):
    return jnp.dot(a, b, preferred_element_type=jnp.float32)


def partial_kernel(me_ref, own, near_top, near_low, other_top, other_low, weight, total):
    me = me_ref[0]
    rows, width = own.shape
    half = rows // 2

    def block_of(source):
        return weight[pl.ds(pl.multiple_of(source * width, width), width), :]

    mine, near, other = block_of(me), block_of(me ^ 1), block_of(3 - me)
    for first, from_near, from_other in ((0, near_top, other_top), (half, near_low, other_low)):
        at = slice(first, first + half)
        total[at, :] = dot(own[at, :], mine) + dot(from_near[...], near) + dot(from_other[...], other)


def last_kernel(me_ref, total, far_top, far_low, weight, *refs):
    base, out = refs[:-1], refs[-1]
    rows, width = total.shape
    half = rows // 2
    block = weight[pl.ds(pl.multiple_of((me_ref[0] ^ 2) * width, width), width), :]
    for first, far in ((0, far_top), (half, far_low)):
        at = slice(first, first + half)
        value = total[at, :] + dot(far[...], block)
        for ref in base:
            value = value + ref[at, :].astype(jnp.float32)
        out[at, :] = value.astype(out.dtype)


def project_by_exchanges(values, weight, base=(), later=None):
    assert lax.axis_size("chan") == 4
    me = lax.axis_index("chan").astype(jnp.int32)[None]
    rows, width = values.shape
    half = rows // 2
    near = functools.partial(exchange, axis="chan", partner=lambda i: i ^ 1)
    other = functools.partial(exchange, axis="chan", partner=lambda i: 3 - i)
    top, low = values[:half], values[half:]
    other_top, near_low = other(top), near(low)
    other_low, near_top = other(low), near(top)
    far_top, far_low = near(other_top), other(near_low)
    params = pltpu.CompilerParams(vmem_limit_bytes=10 << 20)
    total = pl.pallas_call(
        partial_kernel,
        out_shape=jax.ShapeDtypeStruct((rows, width), jnp.float32),
        in_specs=[SMEM] + [VMEM] * 6,
        out_specs=VMEM,
        compiler_params=params,
        cost_estimate=pl.CostEstimate(flops=6 * rows * width * width, bytes_accessed=10 * rows * width, transcendentals=0),
        name="first_blocks",
    )(me, values, near_top, near_low, other_top, other_low, weight)
    if later is not None:
        total, later = lax.optimization_barrier((total, later))
        later = exchange(later, "chan", lambda i: i ^ 2)
    out = pl.pallas_call(
        last_kernel,
        out_shape=jax.ShapeDtypeStruct((rows, width), values.dtype),
        in_specs=[SMEM] + [VMEM] * (4 + len(base)),
        out_specs=VMEM,
        compiler_params=params,
        cost_estimate=pl.CostEstimate(flops=2 * rows * width * width, bytes_accessed=10 * rows * width, transcendentals=0),
        name="last_block",
    )(me, total, far_top, far_low, weight, *base)
    return out, later


def combine_kernel(me_ref, own, near, other, far, first, second, _, mixed, base):
    me, width = me_ref[0], own.shape[1]
    rows, last = own.shape[0], base.shape[0]

    def one_block(start, size, targets):
        at = pl.ds(start, size)
        for column, weight in ((slice(0, width), first), (slice(width, 2 * width), second)):
            value = jnp.zeros((size, width), jnp.float32)
            for source, block in ((me, own), (me ^ 1, near), (3 - me, other), (me ^ 2, far)):
                value += dot(block[at, :], weight[pl.ds(pl.multiple_of(source * width, width), width), :])
            for target, to in targets:
                target[to, column] = value.astype(target.dtype)

    for start in range(0, rows - last, last):
        one_block(start, last, [(mixed, pl.ds(start, last))])
    one_block(rows - last, last, [(base, pl.ds(0, last))])


def combine(blocks, first, second, last, after):
    rows, width = blocks[0].shape
    return pl.pallas_call(
        combine_kernel,
        out_shape=(
            jax.ShapeDtypeStruct((rows - last, 2 * width), blocks[0].dtype),
            jax.ShapeDtypeStruct((last, 2 * width), jnp.float32),
        ),
        in_specs=[SMEM] + [VMEM] * 6 + [HBM],
        out_specs=(VMEM, VMEM),
        compiler_params=pltpu.CompilerParams(vmem_limit_bytes=10 << 20),
        cost_estimate=pl.CostEstimate(flops=16 * rows * width * width, bytes_accessed=16 * rows * width, transcendentals=0),
        name="combine",
    )(lax.axis_index("chan").astype(jnp.int32)[None], *blocks, first, second, after)


def gathered_dot(full, weight):
    depth = full.shape[2]
    return sum(dot(full[j], weight[j * depth : (j + 1) * depth, :]) for j in range(full.shape[0]))


def halves_dot(core, full, mine, other, first, columns):
    half, depth = full.shape[0] // 2, full.shape[2]
    total = 0
    for owner, held in ((core, mine), (1 - core, other)):
        for j in range(half):
            total += dot(full[owner * half + j], held[pl.ds(first + j * depth, depth), columns])
    return total


def mesh_one_kernel(core_ref, full, mesh, w_out, mine, other, base, mesh_one, projected, later):
    core, width = core_ref[0], mesh.shape[1]
    one, two = slice(0, width), slice(width, 2 * width)
    mesh_one[...] = (mesh[...].astype(jnp.float32) + gathered_dot(full, w_out)).astype(mesh_one.dtype)
    projected[...] = (base[:, one] + halves_dot(core, full, mine, other, 0, one)).astype(projected.dtype)
    later[...] = base[:, two] + halves_dot(core, full, mine, other, 0, two)


def mesh_next_kernel(core_ref, full, mesh_one, w_out, mine, other, later, mesh_next, projected):
    width = mesh_one.shape[1]
    first, two = w_out.shape[0] // 2, slice(width, 2 * width)
    mesh_next[...] = (mesh_one[...].astype(jnp.float32) + gathered_dot(full, w_out)).astype(mesh_next.dtype)
    projected[...] = (later[...] + halves_dot(core_ref[0], full, mine, other, first, two)).astype(projected.dtype)


def mesh_step(kernel, like, kinds, core, *operands):
    return pl.pallas_call(
        kernel,
        out_shape=[jax.ShapeDtypeStruct(like.shape, kind) for kind in kinds],
        in_specs=[SMEM] + [VMEM] * len(operands),
        out_specs=[VMEM] * len(kinds),
        compiler_params=pltpu.CompilerParams(vmem_limit_bytes=10 << 20),
        cost_estimate=pl.CostEstimate(flops=len(kinds) << 27, bytes_accessed=1 << 22, transcendentals=0),
        name="mesh_step",
    )(core, *operands)


def window_of_exchanges(projected, later):
    below = shift(projected, 2)
    above = shift(projected, -2)
    other = exchange(projected, "region", lambda i: i ^ 1)
    other, later = lax.optimization_barrier((other, later))
    sent = [exchange(later, "chan", lambda i: i ^ 1), exchange(later, "chan", lambda i: 3 - i)]
    first = lax.axis_index("region") % 2 == 0
    half = projected.shape[0] // 2
    chosen = [jnp.where(first, above[rows], below[rows]) for rows in (slice(0, half), slice(half, None))]
    return [projected, below, above, other] + [core_pair(rows) for rows in chosen], sent


def window_of_pairs(projected):
    below = shift(projected, 2)
    above = shift(projected, -2)
    own = core_pair(projected)
    first = lax.axis_index("region") % 2 == 0
    outer = core_pair(jnp.where(first, above, below))
    last = jnp.where(first, below, above)
    return [outer, own, last]


def edges_kernel(n_grid, n_mesh, me_ref, *refs):
    sources, (first, second, mesh), (o1, s1, o2, s2, o3, s3, packed) = refs[:9], refs[9:12], refs[12:19]
    i1, w1, c1, i2, w2, c2, i3, w3, c3 = held = refs[19:28]
    semaphores = refs[28]
    me = me_ref[0]
    half = first.shape[0] // 2
    mine = pl.ds(pl.multiple_of((me & 1) * half, half), half)
    moves = list(zip(sources, held)) + [
        (first.at[mine, :], packed.at[pl.ds(0, half), :]),
        (second.at[mine, :], packed.at[pl.ds(half, half), :]),
        (mesh, packed.at[pl.ds(2 * half, mesh.shape[0]), :]),
    ]
    copies = [pltpu.make_async_copy(src, dst, semaphores.at[k]) for k, (src, dst) in enumerate(moves)]
    for copy in copies:
        copy.start()
    for copy in copies:
        copy.wait()
    core = me & 1

    def of_exchanges(apart):
        towards = 1 - 2 * core
        return jnp.where(apart == 0, 0, jnp.where(apart == -2, 1, jnp.where(apart == 2, 2, jnp.where(apart == towards, 3, 4))))

    def of_pairs(apart):
        apart = apart + core
        return jnp.where(apart == 2, 0, jnp.where(apart == -1, 1, jnp.where(apart == 0, 2, jnp.where(apart == 1, 3, 4))))

    def place(index, rows, piece):
        shift_by = rows.bit_length() - 1
        return (piece((index >> shift_by) - me) << shift_by) + (index & (rows - 1))

    def halved(at, rows):
        row, half = at - 4 * rows, rows // 2
        moved = 4 * rows + jnp.where(row < half, row, row + half) + (1 - core) * half
        return jnp.where(row < 0, at, moved)

    def scaled(w, c):
        live = lax.broadcasted_iota(jnp.int32, w.shape, 0) < c[...]
        return jnp.where(live, w[...], 0.0) / c[...].astype(jnp.float32)

    def upright(v):
        if v.shape[0] < TILE:
            v = jnp.concatenate([v, jnp.zeros((TILE - v.shape[0], v.shape[1]), v.dtype)], axis=0)
        return v.T

    o1[...] = 2 * halved(place(i1[...], n_grid, of_exchanges), n_grid)
    tall = upright(scaled(w1, c1))
    for s in range(2):
        s1[pl.ds(s, tall.shape[0], 2), :] = tall
    o2[...] = upright(place(i2[...], n_mesh, of_pairs))
    s2[...] = upright(scaled(w2, c2))
    o3[...] = upright(place(i3[...], n_mesh, of_pairs))
    s3[...] = upright(scaled(w3, c3))


def edges(n_grid, n_mesh, g2m, m2m, m2g, first, second, mesh):
    me = lax.axis_index("region").astype(jnp.int32)[None]
    ops, outs = [me], []
    for at, (index, weight, count) in enumerate((g2m, m2m, m2g)):
        slots, rows = index.shape
        ops += [index, weight, count[None, :]]
        high = max(slots, TILE)
        outs += [
            jax.ShapeDtypeStruct((slots, rows) if at == 0 else (rows, high), jnp.int32),
            jax.ShapeDtypeStruct((2 * rows if at == 0 else rows, high), jnp.float32),
        ]
    packed = (first.shape[0] + mesh.shape[0], mesh.shape[1])
    outs.append(jax.ShapeDtypeStruct(packed, mesh.dtype))
    return pl.pallas_call(
        functools.partial(edges_kernel, n_grid, n_mesh),
        out_shape=outs,
        in_specs=[SMEM] + [HBM] * 12,
        out_specs=[VMEM] * 7,
        scratch_shapes=[pltpu.VMEM(op.shape, op.dtype) for op in ops[1:]] + [pltpu.SemaphoreType.DMA((12,))],
        compiler_params=pltpu.CompilerParams(vmem_limit_bytes=60 << 20),
        cost_estimate=pl.CostEstimate(flops=1 << 20, bytes_accessed=1 << 20, transcendentals=0),
        name="edges",
    )(*ops, first, second, mesh)


def by_rows_kernel(slots, rows, group, sizes, index_ref, weight_ref, receiver_ref, *refs):
    parts, out_ref = refs[: len(sizes)], refs[len(sizes)]
    window, receiver, fetched, total = refs[len(sizes) + 1 :]
    first = 0
    for part, size in zip(parts, sizes):
        half = part[...].astype(jnp.float32) * 0.5
        for s in range(2):
            window[pl.ds(2 * first + s, size, 2), :] = half[:, s * LANES : (s + 1) * LANES]
        first += size
    half = receiver_ref[...].astype(jnp.float32) * 0.5
    for s in range(2):
        receiver[pl.ds(s, rows, 2), :] = half[:, s * LANES : (s + 1) * LANES]

    def fetch(start, side):
        for u in range(group):
            for k in range(slots):
                at = ((u // 4) * slots + k) * TILE + (u % 4) * 2
                fetched[side, at : at + 2, :] = window[pl.ds(index_ref[k, start + u], 2), :]

    def add_up(start, side):
        for t in range(group // 4):
            row = pl.multiple_of(2 * start + TILE * t, TILE)
            mine = receiver[pl.ds(row, TILE), :]
            weight = weight_ref[pl.ds(row, TILE), :]
            acc = jnp.zeros((TILE, LANES), jnp.float32)
            for k in range(slots):
                at = (t * slots + k) * TILE
                h = fetched[side, at : at + TILE, :] + mine
                acc = acc + (h + h * jnp.tanh(h)) * weight[:, k : k + 1]
            total[pl.ds(row, TILE), :] = acc

    fetch(0, 0)

    def two_groups(j, carry):
        start = j * 2 * group
        fetch(start + group, 1)
        add_up(start, 0)
        fetch(jnp.minimum(start + 2 * group, rows - group), 0)
        add_up(start + group, 1)
        return carry

    lax.fori_loop(0, rows // (2 * group), two_groups, 0)
    for s in range(2):
        value = total[pl.ds(s, rows, 2), :].astype(out_ref.dtype)
        for j in range(out_ref.shape[0]):
            out_ref[j, :, s * LANES : (s + 1) * LANES] = value


def aggregate_by_rows(index, weights, receivers, parts, copies, group=8):
    slots, rows = index.shape
    width = receivers.shape[1]
    sizes = tuple(part.shape[0] for part in parts)
    return pl.pallas_call(
        functools.partial(by_rows_kernel, slots, rows, group, sizes),
        out_shape=jax.ShapeDtypeStruct((copies, rows, width), receivers.dtype),
        in_specs=[SMEM] + [VMEM] * (2 + len(parts)),
        out_specs=VMEM,
        scratch_shapes=[
            pltpu.VMEM((2 * sum(sizes), LANES), jnp.float32),
            pltpu.VMEM((2 * rows, LANES), jnp.float32),
            pltpu.VMEM((2, group // 4 * slots * TILE, LANES), jnp.float32),
            pltpu.VMEM((2 * rows, LANES), jnp.float32),
        ],
        compiler_params=pltpu.CompilerParams(vmem_limit_bytes=14 << 20),
        cost_estimate=pl.CostEstimate(flops=1, bytes_accessed=1, transcendentals=0),
        name="aggregate_by_rows",
    )(index, weights, receivers, *parts)


def by_matmul_kernel(slots, rows, block, sizes, index_ref, weight_ref, receiver_ref, *refs):
    parts, out_ref, window = refs[: len(sizes)], refs[len(sizes)], refs[len(sizes) + 1]
    first = 0
    for part, size in zip(parts, sizes):
        window[first : first + size, :] = part[...]
        first += size
    columns = lax.broadcasted_iota(jnp.int32, (block, first), 1).astype(jnp.int16)
    one, zero = jnp.bfloat16(1), jnp.bfloat16(0)

    def one_block(b, carry):
        at = pl.ds(pl.multiple_of(b * block, block), block)
        mine = receiver_ref[at, :].astype(jnp.float32)
        index, weight = index_ref[at, :], weight_ref[at, :]
        acc = jnp.zeros(mine.shape, jnp.float32)
        for k in range(slots):
            wanted = jnp.broadcast_to(index[:, k : k + 1], (block, LANES)).astype(jnp.int16)
            pick = [jnp.where(columns[:, j : j + LANES] == wanted, one, zero) for j in range(0, first, LANES)]
            fetched = dot(jnp.concatenate(pick, axis=1), window[...])
            h = (fetched + mine) * 0.5
            acc = acc + (h + h * jnp.tanh(h)) * weight[:, k : k + 1]
        for j in range(out_ref.shape[0]):
            out_ref[j, at, :] = acc.astype(out_ref.dtype)
        return carry

    lax.fori_loop(0, rows // block, one_block, 0)


def aggregate_by_matmul(slots, index, weights, receivers, parts, copies, block=256):
    rows, width = receivers.shape
    sizes = tuple(part.shape[0] for part in parts)
    return pl.pallas_call(
        functools.partial(by_matmul_kernel, slots, rows, block, sizes),
        out_shape=jax.ShapeDtypeStruct((copies, rows, width), receivers.dtype),
        in_specs=[VMEM] * (3 + len(parts)),
        out_specs=VMEM,
        scratch_shapes=[pltpu.VMEM((sum(sizes), width), jnp.bfloat16)],
        compiler_params=pltpu.CompilerParams(vmem_limit_bytes=14 << 20),
        cost_estimate=pl.CostEstimate(
            flops=2 * slots * rows * sum(sizes) * width,
            bytes_accessed=2 * width * (sum(sizes) + 2 * rows),
            transcendentals=slots * rows * width,
        ),
        name="aggregate_by_matmul",
    )(index, weights, receivers, *parts)


def shards(
    grid_state,
    mesh_state,
    enc_send,
    enc_out,
    proc_send,
    proc_out,
    dec_send,
    dec_out,
    g2m_index,
    g2m_weight,
    g2m_count,
    m2m_index,
    m2m_weight,
    m2m_count,
    m2g_index,
    m2g_weight,
    m2g_count,
):
    n_grid, n_mesh = grid_state.shape[0], mesh_state.shape[0]
    bf16, f32 = jnp.bfloat16, jnp.float32
    k_m, k_d = m2m_index.shape[0], m2g_index.shape[0]
    core = lax.axis_index("region").astype(jnp.int32) % 2
    prepared = edges(
        n_grid,
        n_mesh,
        (g2m_index, g2m_weight, g2m_count),
        (m2m_index, m2m_weight, m2m_count),
        (m2g_index, m2g_weight, m2g_count),
        enc_out,
        proc_out,
        mesh_state,
    )
    grid_state, prepared = lax.optimization_barrier((grid_state, prepared))
    g2m, g2m_w, m2m, m2m_w, m2g, m2g_w, packed = prepared

    projected, far = project_by_exchanges(grid_state, enc_send, later=packed)
    window, nearer = window_of_exchanges(projected, packed)
    n = lax.axis_size("chan")
    agg = aggregate_by_rows(g2m, g2m_w, mesh_state, window, 1)

    full = lax.all_gather(agg[0], "chan", axis=0)
    mine, base = combine([packed, *nearer, far], proc_send, dec_send, n_mesh, full)
    other = exchange(mine, "region", lambda i: i ^ 1)
    mesh_one, projected, later = mesh_step(
        mesh_one_kernel, mesh_state, (bf16, bf16, f32), core[None], full, mesh_state, enc_out, mine, other, base
    )
    agg = aggregate_by_matmul(k_m, m2m, m2m_w, mesh_one, window_of_pairs(projected), n)
    mesh_next, projected = mesh_step(
        mesh_next_kernel, mesh_state, (bf16, bf16), core[None], gather_chan(agg), mesh_one, proc_out, mine, other, later
    )
    agg = aggregate_by_matmul(k_d, m2g, m2g_w, grid_state, window_of_pairs(projected), 1)[0]
    grid_next, _ = project_by_exchanges(agg, dec_out, base=(grid_state,))
    return grid_next, mesh_next


def solution(mesh):
    by_both, by_chan = P("region", "chan"), P(None, "chan")
    edge = (P(None, "region"), P(None, "region"), P("region"))
    return jax.shard_map(
        shards,
        mesh=mesh,
        in_specs=(by_both,) * 2 + (by_chan,) * 6 + edge * 3,
        out_specs=(by_both, by_both),
        check_vma=False,
    )
```

```python
import functools

import jax
import jax.numpy as jnp
from jax import lax
from jax.experimental import pallas as pl
from jax.experimental.pallas import tpu as pltpu
from jax.sharding import PartitionSpec as P

LANES = 128
TILE = 8
VMEM = pl.BlockSpec(memory_space=pltpu.VMEM)
HBM = pl.BlockSpec(memory_space=pltpu.HBM)
SMEM = pl.BlockSpec(memory_space=pltpu.SMEM)


def exchange(shard, axis, partner):
    n = lax.axis_size(axis)
    return lax.ppermute(shard, axis, [(i, partner(i)) for i in range(n)])


def shift(shard, by):
    n = lax.axis_size("region")
    return lax.ppermute(shard, "region", [(i, i + by) for i in range(n) if 0 <= i + by < n])


def core_pair(shard):
    n = lax.axis_size("region")
    groups = [[i, i + 1] for i in range(0, n, 2)]
    return lax.all_gather(shard, "region", axis=0, tiled=True, axis_index_groups=groups)


def gather_chan(copies):
    return lax.all_to_all(copies, "chan", split_axis=0, concat_axis=0, tiled=True)


def dot(a, b):
    return jnp.dot(a, b, preferred_element_type=jnp.float32)


def partial_kernel(me_ref, own, near_top, near_low, other_top, other_low, weight, total):
    me = me_ref[0]
    rows, width = own.shape
    half = rows // 2

    def block_of(source):
        return weight[pl.ds(pl.multiple_of(source * width, width), width), :]

    mine, near, other = block_of(me), block_of(me ^ 1), block_of(3 - me)
    for first, from_near, from_other in ((0, near_top, other_top), (half, near_low, other_low)):
        at = slice(first, first + half)
        total[at, :] = dot(own[at, :], mine) + dot(from_near[...], near) + dot(from_other[...], other)


def last_kernel(me_ref, total, far_top, far_low, weight, *refs):
    base, out = refs[:-1], refs[-1]
    rows, width = total.shape
    half = rows // 2
    block = weight[pl.ds(pl.multiple_of((me_ref[0] ^ 2) * width, width), width), :]
    for first, far in ((0, far_top), (half, far_low)):
        at = slice(first, first + half)
        value = total[at, :] + dot(far[...], block)
        for ref in base:
            value = value + ref[at, :].astype(jnp.float32)
        out[at, :] = value.astype(out.dtype)


def project_by_exchanges(values, weight, base=(), later=None):
    assert lax.axis_size("chan") == 4
    me = lax.axis_index("chan").astype(jnp.int32)[None]
    rows, width = values.shape
    half = rows // 2
    near = functools.partial(exchange, axis="chan", partner=lambda i: i ^ 1)
    other = functools.partial(exchange, axis="chan", partner=lambda i: 3 - i)
    top, low = values[:half], values[half:]
    other_top, near_low = other(top), near(low)
    other_low, near_top = other(low), near(top)
    far_top, far_low = near(other_top), other(near_low)
    params = pltpu.CompilerParams(vmem_limit_bytes=10 << 20)
    total = pl.pallas_call(
        partial_kernel,
        out_shape=jax.ShapeDtypeStruct((rows, width), jnp.float32),
        in_specs=[SMEM] + [VMEM] * 6,
        out_specs=VMEM,
        compiler_params=params,
        cost_estimate=pl.CostEstimate(flops=6 * rows * width * width, bytes_accessed=10 * rows * width, transcendentals=0),
        name="first_blocks",
    )(me, values, near_top, near_low, other_top, other_low, weight)
    if later is not None:
        total, later = lax.optimization_barrier((total, later))
        later = exchange(later, "chan", lambda i: i ^ 2)
    out = pl.pallas_call(
        last_kernel,
        out_shape=jax.ShapeDtypeStruct((rows, width), values.dtype),
        in_specs=[SMEM] + [VMEM] * (4 + len(base)),
        out_specs=VMEM,
        compiler_params=params,
        cost_estimate=pl.CostEstimate(flops=2 * rows * width * width, bytes_accessed=10 * rows * width, transcendentals=0),
        name="last_block",
    )(me, total, far_top, far_low, weight, *base)
    return out, later


def combine_kernel(me_ref, own, near, other, far, first, second, _, mixed, base):
    me, width = me_ref[0], own.shape[1]
    rows, last = own.shape[0], base.shape[0]
    half = (rows - last) // 2
    blocks = [(me, own), (me ^ 1, near), (3 - me, other), (me ^ 2, far)]

    def product(start, size, weight):
        value = jnp.zeros((size, width), jnp.float32)
        for source, block in blocks:
            value += dot(block[pl.ds(start, size), :], weight[pl.ds(pl.multiple_of(source * width, width), width), :])
        return value

    for section, start, weight in ((0, 0, first), (1, 0, second), (2, half, second)):
        mixed[pl.ds(section * half, half), :] = product(start, half, weight).astype(mixed.dtype)
    base[:, :width] = product(2 * half, last, first)
    base[:, width:] = product(2 * half, last, second)


def combine(blocks, first, second, last, after):
    rows, width = blocks[0].shape
    return pl.pallas_call(
        combine_kernel,
        out_shape=(
            jax.ShapeDtypeStruct(((rows - last) // 2 * 3, width), blocks[0].dtype),
            jax.ShapeDtypeStruct((last, 2 * width), jnp.float32),
        ),
        in_specs=[SMEM] + [VMEM] * 6 + [HBM],
        out_specs=(VMEM, VMEM),
        compiler_params=pltpu.CompilerParams(vmem_limit_bytes=10 << 20),
        cost_estimate=pl.CostEstimate(flops=16 * rows * width * width, bytes_accessed=16 * rows * width, transcendentals=0),
        name="combine",
    )(lax.axis_index("chan").astype(jnp.int32)[None], *blocks, first, second, after)


def gathered_dot(full, weight):
    depth = full.shape[2]
    return sum(dot(full[j], weight[j * depth : (j + 1) * depth, :]) for j in range(full.shape[0]))


def halves_dot(core, full, mine, other, section):
    half, depth = full.shape[0] // 2, full.shape[2]
    total = 0
    for owner, held in ((core, mine), (1 - core, other)):
        for j in range(half):
            total += dot(full[owner * half + j], held[pl.ds((section * half + j) * depth, depth), :])
    return total


def mesh_one_kernel(core_ref, full, mesh, w_out, mine, other, base, mesh_one, projected, later):
    core, width = core_ref[0], mesh.shape[1]
    mesh_one[...] = (mesh[...].astype(jnp.float32) + gathered_dot(full, w_out)).astype(mesh_one.dtype)
    projected[...] = (base[:, :width] + halves_dot(core, full, mine, other, 0)).astype(projected.dtype)
    later[...] = base[:, width:] + halves_dot(core, full, mine, other, 1)


def mesh_next_kernel(core_ref, full, mesh_one, w_out, mine, other, later, mesh_next, projected):
    mesh_next[...] = (mesh_one[...].astype(jnp.float32) + gathered_dot(full, w_out)).astype(mesh_next.dtype)
    projected[...] = (later[...] + halves_dot(core_ref[0], full, mine, other, 2)).astype(projected.dtype)


def mesh_step(kernel, like, kinds, core, *operands):
    return pl.pallas_call(
        kernel,
        out_shape=[jax.ShapeDtypeStruct(like.shape, kind) for kind in kinds],
        in_specs=[SMEM] + [VMEM] * len(operands),
        out_specs=[VMEM] * len(kinds),
        compiler_params=pltpu.CompilerParams(vmem_limit_bytes=10 << 20),
        cost_estimate=pl.CostEstimate(flops=len(kinds) << 27, bytes_accessed=1 << 22, transcendentals=0),
        name="mesh_step",
    )(core, *operands)


def window_of_exchanges(projected, later):
    below = shift(projected, 2)
    above = shift(projected, -2)
    other = exchange(projected, "region", lambda i: i ^ 1)
    other, later = lax.optimization_barrier((other, later))
    sent = [exchange(later, "chan", lambda i: i ^ 1), exchange(later, "chan", lambda i: 3 - i)]
    first = lax.axis_index("region") % 2 == 0
    half = projected.shape[0] // 2
    chosen = [jnp.where(first, above[rows], below[rows]) for rows in (slice(0, half), slice(half, None))]
    return [projected, below, above, other] + [core_pair(rows) for rows in chosen], sent


def window_of_pairs(projected, fetch_own):
    below = shift(projected, 2)
    above = shift(projected, -2)
    fetched = fetch_own(core_pair(projected))
    above, fetched = lax.optimization_barrier((above, fetched))
    first = lax.axis_index("region") % 2 == 0
    outer = core_pair(jnp.where(first, above, below))
    last = jnp.where(first, below, above)
    return fetched, [outer, last]


def place_in_exchanged(index, rows, me):
    core = me & 1
    apart, row = index // rows - me, index % rows
    block = jnp.where(apart == 0, 0, jnp.where(apart == -2, 1, jnp.where(apart == 2, 2, 3)))
    half = rows // 2
    moved = 4 * rows + jnp.where(row < half, row, row + half) + (1 - core) * half
    near = (apart == 0) | (apart == 1 - 2 * core) | (apart == 2) | (apart == -2)
    return jnp.where(near, block * rows + row, moved)


def place_in_pairs(index, rows, me, own):
    shift_by = rows.bit_length() - 1
    apart = (index >> shift_by) - (me - (me & 1))
    inside = (apart == 0) | (apart == 1)
    if own:
        block = jnp.where(inside, apart, 2)
    else:
        block = jnp.where(inside, 3, jnp.where(apart == 2, 0, jnp.where(apart == -1, 1, 2)))
    return (block << shift_by) + (index & (rows - 1))


def scaled(weight, count):
    live = lax.broadcasted_iota(jnp.int32, weight.shape, 0) < count
    return jnp.where(live, weight, 0.0) / count.astype(jnp.float32)


def upright(v):
    if v.shape[0] < TILE:
        v = jnp.concatenate([v, jnp.zeros((TILE - v.shape[0], v.shape[1]), v.dtype)], axis=0)
    return v.T


def by_rows_kernel(slots, rows, group, sizes, index_ref, slot_ref, count_ref, receiver_ref, *refs):
    parts, out_ref = refs[: len(sizes)], refs[len(sizes)]
    window, receiver, fetched, total, weight_ref = refs[len(sizes) + 1 :]
    tall = upright(scaled(slot_ref[...], count_ref[...]))
    for s in range(2):
        weight_ref[pl.ds(s, rows, 2), :] = tall
    first = 0
    for part, size in zip(parts, sizes):
        half = part[...].astype(jnp.float32) * 0.5
        for s in range(2):
            window[pl.ds(2 * first + s, size, 2), :] = half[:, s * LANES : (s + 1) * LANES]
        first += size
    half = receiver_ref[...].astype(jnp.float32) * 0.5
    for s in range(2):
        receiver[pl.ds(s, rows, 2), :] = half[:, s * LANES : (s + 1) * LANES]

    def fetch(start, side):
        for u in range(group):
            for k in range(slots):
                at = ((u // 4) * slots + k) * TILE + (u % 4) * 2
                fetched[side, at : at + 2, :] = window[pl.ds(index_ref[k, start + u], 2), :]

    def add_up(start, side):
        for t in range(group // 4):
            row = pl.multiple_of(2 * start + TILE * t, TILE)
            mine = receiver[pl.ds(row, TILE), :]
            weight = weight_ref[pl.ds(row, TILE), :]
            acc = jnp.zeros((TILE, LANES), jnp.float32)
            for k in range(slots):
                at = (t * slots + k) * TILE
                h = fetched[side, at : at + TILE, :] + mine
                acc = acc + (h + h * jnp.tanh(h)) * weight[:, k : k + 1]
            total[pl.ds(row, TILE), :] = acc

    fetch(0, 0)

    def two_groups(j, carry):
        start = j * 2 * group
        fetch(start + group, 1)
        add_up(start, 0)
        fetch(jnp.minimum(start + 2 * group, rows - group), 0)
        add_up(start + group, 1)
        return carry

    lax.fori_loop(0, rows // (2 * group), two_groups, 0)
    for s in range(2):
        value = total[pl.ds(s, rows, 2), :].astype(out_ref.dtype)
        for j in range(out_ref.shape[0]):
            out_ref[j, :, s * LANES : (s + 1) * LANES] = value


def aggregate_by_rows(index, weights, counts, receivers, parts, copies, group=8):
    slots, rows = index.shape
    width = receivers.shape[1]
    sizes = tuple(part.shape[0] for part in parts)
    return pl.pallas_call(
        functools.partial(by_rows_kernel, slots, rows, group, sizes),
        out_shape=jax.ShapeDtypeStruct((copies, rows, width), receivers.dtype),
        in_specs=[SMEM] + [VMEM] * (3 + len(parts)),
        out_specs=VMEM,
        scratch_shapes=[
            pltpu.VMEM((2 * sum(sizes), LANES), jnp.float32),
            pltpu.VMEM((2 * rows, LANES), jnp.float32),
            pltpu.VMEM((2, group // 4 * slots * TILE, LANES), jnp.float32),
            pltpu.VMEM((2 * rows, LANES), jnp.float32),
            pltpu.VMEM((2 * rows, slots), jnp.float32),
        ],
        compiler_params=pltpu.CompilerParams(vmem_limit_bytes=14 << 20),
        cost_estimate=pl.CostEstimate(flops=1, bytes_accessed=1, transcendentals=0),
        name="aggregate_by_rows",
    )(index, weights, counts[None, :], receivers, *parts)


def pick_rows(index, columns, window):
    wanted = jnp.broadcast_to(index, (index.shape[0], LANES)).astype(jnp.int16)
    one, zero = jnp.bfloat16(1), jnp.bfloat16(0)
    picks = [jnp.where(columns[:, j : j + LANES] == wanted, one, zero) for j in range(0, columns.shape[1], LANES)]
    return dot(jnp.concatenate(picks, axis=1), window[...])


def fetch_kernel(slots, block, me_ref, sender_ref, window, out_ref, index_ref):
    depth, rows = window.shape[0], sender_ref.shape[1]
    index_ref[...] = upright(place_in_pairs(sender_ref[...], depth // 2, me_ref[0], True))
    columns = lax.broadcasted_iota(jnp.int32, (block, depth), 1).astype(jnp.int16)

    def one_block(b, carry):
        at = pl.ds(pl.multiple_of(b * block, block), block)
        index = index_ref[at, :]
        for k in range(slots):
            out_ref[k, at, :] = pick_rows(index[:, k : k + 1], columns, window).astype(out_ref.dtype)
        return carry

    lax.fori_loop(0, rows // block, one_block, 0)


def fetch_own(senders, window, block=256):
    slots, rows = senders.shape
    width = window.shape[1]
    me = lax.axis_index("region").astype(jnp.int32)[None]
    return pl.pallas_call(
        functools.partial(fetch_kernel, slots, block),
        out_shape=jax.ShapeDtypeStruct((slots, rows, width), window.dtype),
        in_specs=[SMEM, VMEM, VMEM],
        out_specs=VMEM,
        scratch_shapes=[pltpu.VMEM((rows, max(slots, TILE)), jnp.int32)],
        compiler_params=pltpu.CompilerParams(vmem_limit_bytes=10 << 20),
        cost_estimate=pl.CostEstimate(
            flops=2 * slots * rows * window.shape[0] * width, bytes_accessed=2 * slots * rows * width, transcendentals=0
        ),
        name="fetch_own",
    )(me, senders, window)


def by_matmul_kernel(slots, block, sizes, me_ref, sender_ref, slot_ref, count_ref, receiver_ref, fetched_ref, *refs):
    parts, out_ref = refs[: len(sizes)], refs[len(sizes)]
    window, index_ref, weight_ref = refs[len(sizes) + 1 :]
    depth, rows = sum(sizes), sender_ref.shape[1]
    index_ref[...] = upright(place_in_pairs(sender_ref[...], depth // 3, me_ref[0], False))
    weight_ref[...] = upright(scaled(slot_ref[...], count_ref[...]))
    first = 0
    for part, size in zip(parts, sizes):
        window[first : first + size, :] = part[...]
        first += size
    columns = lax.broadcasted_iota(jnp.int32, (block, depth), 1).astype(jnp.int16)

    def one_block(b, carry):
        at = pl.ds(pl.multiple_of(b * block, block), block)
        mine = receiver_ref[at, :].astype(jnp.float32)
        index, weight = index_ref[at, :], weight_ref[at, :]
        acc = jnp.zeros(mine.shape, jnp.float32)
        for k in range(slots):
            fetched = pick_rows(index[:, k : k + 1], columns, window) + fetched_ref[k, at, :].astype(jnp.float32)
            h = (fetched + mine) * 0.5
            acc = acc + (h + h * jnp.tanh(h)) * weight[:, k : k + 1]
        for j in range(out_ref.shape[0]):
            out_ref[j, at, :] = acc.astype(out_ref.dtype)
        return carry

    lax.fori_loop(0, rows // block, one_block, 0)


def aggregate_by_matmul(senders, weights, counts, receivers, projected, copies, block=256):
    slots, (rows, width) = senders.shape[0], receivers.shape
    me = lax.axis_index("region").astype(jnp.int32)[None]
    fetched, parts = window_of_pairs(projected, functools.partial(fetch_own, senders))
    sizes = tuple(part.shape[0] for part in parts)
    return pl.pallas_call(
        functools.partial(by_matmul_kernel, slots, block, sizes),
        out_shape=jax.ShapeDtypeStruct((copies, rows, width), receivers.dtype),
        in_specs=[SMEM] + [VMEM] * (5 + len(parts)),
        out_specs=VMEM,
        scratch_shapes=[
            pltpu.VMEM((sum(sizes), width), jnp.bfloat16),
            pltpu.VMEM((rows, max(slots, TILE)), jnp.int32),
            pltpu.VMEM((rows, max(slots, TILE)), jnp.float32),
        ],
        compiler_params=pltpu.CompilerParams(vmem_limit_bytes=14 << 20),
        cost_estimate=pl.CostEstimate(
            flops=2 * slots * rows * sum(sizes) * width,
            bytes_accessed=2 * width * (sum(sizes) + 2 * rows),
            transcendentals=slots * rows * width,
        ),
        name="aggregate_by_matmul",
    )(me, senders, weights, counts[None, :], receivers, fetched, *parts)


def shards(
    grid_state,
    mesh_state,
    enc_send,
    enc_out,
    proc_send,
    proc_out,
    dec_send,
    dec_out,
    g2m_index,
    g2m_weight,
    g2m_count,
    m2m_index,
    m2m_weight,
    m2m_count,
    m2g_index,
    m2g_weight,
    m2g_count,
):
    n_grid, n_mesh = grid_state.shape[0], mesh_state.shape[0]
    bf16, f32 = jnp.bfloat16, jnp.float32
    core = lax.axis_index("region").astype(jnp.int32) % 2
    half = enc_out.shape[0] // 2
    own_rows = [lax.dynamic_slice_in_dim(w, core * half, half, axis=0) for w in (enc_out, proc_out)]
    packed = jnp.concatenate(own_rows + [mesh_state], axis=0)
    g2m = 2 * place_in_exchanged(g2m_index, n_grid, lax.axis_index("region").astype(jnp.int32))

    projected, far = project_by_exchanges(grid_state, enc_send, later=packed)
    window, nearer = window_of_exchanges(projected, packed)
    n = lax.axis_size("chan")
    agg = aggregate_by_rows(g2m, g2m_weight, g2m_count, mesh_state, window, 1)

    full = lax.all_gather(agg[0], "chan", axis=0)
    mine, base = combine([packed, *nearer, far], proc_send, dec_send, n_mesh, full)
    other = exchange(mine, "region", lambda i: i ^ 1)
    mesh_one, projected, later = mesh_step(
        mesh_one_kernel, mesh_state, (bf16, bf16, f32), core[None], full, mesh_state, enc_out, mine, other, base
    )
    agg = aggregate_by_matmul(m2m_index, m2m_weight, m2m_count, mesh_one, projected, n)
    mesh_next, projected = mesh_step(
        mesh_next_kernel, mesh_state, (bf16, bf16), core[None], gather_chan(agg), mesh_one, proc_out, mine, other, later
    )
    agg = aggregate_by_matmul(m2g_index, m2g_weight, m2g_count, grid_state, projected, 1)[0]
    grid_next, _ = project_by_exchanges(agg, dec_out, base=(grid_state,))
    return grid_next, mesh_next


def solution(mesh):
    by_both, by_chan = P("region", "chan"), P(None, "chan")
    edge = (P(None, "region"), P(None, "region"), P("region"))
    return jax.shard_map(
        shards,
        mesh=mesh,
        in_specs=(by_both,) * 2 + (by_chan,) * 6 + edge * 3,
        out_specs=(by_both, by_both),
        check_vma=False,
    )
```

```python
import functools

import jax
import jax.numpy as jnp
from jax import lax
from jax.experimental import pallas as pl
from jax.experimental.pallas import tpu as pltpu
from jax.sharding import PartitionSpec as P

LANES = 128
TILE = 8
VMEM = pl.BlockSpec(memory_space=pltpu.VMEM)
HBM = pl.BlockSpec(memory_space=pltpu.HBM)
SMEM = pl.BlockSpec(memory_space=pltpu.SMEM)


def exchange(shard, axis, partner):
    n = lax.axis_size(axis)
    return lax.ppermute(shard, axis, [(i, partner(i)) for i in range(n)])


def shift(shard, by):
    n = lax.axis_size("region")
    return lax.ppermute(shard, "region", [(i, i + by) for i in range(n) if 0 <= i + by < n])


def core_pair(shard):
    n = lax.axis_size("region")
    groups = [[i, i + 1] for i in range(0, n, 2)]
    return lax.all_gather(shard, "region", axis=0, tiled=True, axis_index_groups=groups)


def gather_chan(copies):
    return lax.all_to_all(copies, "chan", split_axis=0, concat_axis=0, tiled=True)


def dot(a, b):
    return jnp.dot(a, b, preferred_element_type=jnp.float32)


def partial_kernel(me_ref, own, near_top, near_low, other_top, other_low, weight, total):
    me = me_ref[0]
    rows, width = own.shape
    half = rows // 2

    def block_of(source):
        return weight[pl.ds(pl.multiple_of(source * width, width), width), :]

    mine, near, other = block_of(me), block_of(me ^ 1), block_of(3 - me)
    for first, from_near, from_other in ((0, near_top, other_top), (half, near_low, other_low)):
        at = slice(first, first + half)
        total[at, :] = dot(own[at, :], mine) + dot(from_near[...], near) + dot(from_other[...], other)


def last_kernel(me_ref, total, far_top, far_low, weight, *refs):
    base, out = refs[:-1], refs[-1]
    rows, width = total.shape
    half = rows // 2
    block = weight[pl.ds(pl.multiple_of((me_ref[0] ^ 2) * width, width), width), :]
    for first, far in ((0, far_top), (half, far_low)):
        at = slice(first, first + half)
        value = total[at, :] + dot(far[...], block)
        for ref in base:
            value = value + ref[at, :].astype(jnp.float32)
        out[at, :] = value.astype(out.dtype)


def project_by_exchanges(values, weight, base=(), later=None):
    assert lax.axis_size("chan") == 4
    me = lax.axis_index("chan").astype(jnp.int32)[None]
    rows, width = values.shape
    half = rows // 2
    near = functools.partial(exchange, axis="chan", partner=lambda i: i ^ 1)
    other = functools.partial(exchange, axis="chan", partner=lambda i: 3 - i)
    top, low = values[:half], values[half:]
    other_top, near_low = other(top), near(low)
    other_low, near_top = other(low), near(top)
    far_top, far_low = near(other_top), other(near_low)
    params = pltpu.CompilerParams(vmem_limit_bytes=10 << 20)
    total = pl.pallas_call(
        partial_kernel,
        out_shape=jax.ShapeDtypeStruct((rows, width), jnp.float32),
        in_specs=[SMEM] + [VMEM] * 6,
        out_specs=VMEM,
        compiler_params=params,
        cost_estimate=pl.CostEstimate(flops=6 * rows * width * width, bytes_accessed=10 * rows * width, transcendentals=0),
        name="first_blocks",
    )(me, values, near_top, near_low, other_top, other_low, weight)
    if later is not None:
        total, later = lax.optimization_barrier((total, later))
        later = exchange(later, "chan", lambda i: i ^ 2)
    out = pl.pallas_call(
        last_kernel,
        out_shape=jax.ShapeDtypeStruct((rows, width), values.dtype),
        in_specs=[SMEM] + [VMEM] * (4 + len(base)),
        out_specs=VMEM,
        compiler_params=params,
        cost_estimate=pl.CostEstimate(flops=2 * rows * width * width, bytes_accessed=10 * rows * width, transcendentals=0),
        name="last_block",
    )(me, total, far_top, far_low, weight, *base)
    return out, later


def combine_kernel(me_ref, own, near, other, far, first, second, _, mixed, base):
    me, width = me_ref[0], own.shape[1]
    rows, last = own.shape[0], base.shape[0]
    half = (rows - last) // 2
    blocks = [(me, own), (me ^ 1, near), (3 - me, other), (me ^ 2, far)]

    def product(start, size, weight):
        value = jnp.zeros((size, width), jnp.float32)
        for source, block in blocks:
            value += dot(block[pl.ds(start, size), :], weight[pl.ds(pl.multiple_of(source * width, width), width), :])
        return value

    for section, start, weight in ((0, 0, first), (1, 0, second), (2, half, second)):
        mixed[pl.ds(section * half, half), :] = product(start, half, weight).astype(mixed.dtype)
    base[:, :width] = product(2 * half, last, first)
    base[:, width:] = product(2 * half, last, second)


def combine(blocks, first, second, last, after):
    rows, width = blocks[0].shape
    return pl.pallas_call(
        combine_kernel,
        out_shape=(
            jax.ShapeDtypeStruct(((rows - last) // 2 * 3, width), blocks[0].dtype),
            jax.ShapeDtypeStruct((last, 2 * width), jnp.float32),
        ),
        in_specs=[SMEM] + [VMEM] * 6 + [HBM],
        out_specs=(VMEM, VMEM),
        compiler_params=pltpu.CompilerParams(vmem_limit_bytes=10 << 20),
        cost_estimate=pl.CostEstimate(flops=16 * rows * width * width, bytes_accessed=16 * rows * width, transcendentals=0),
        name="combine",
    )(lax.axis_index("chan").astype(jnp.int32)[None], *blocks, first, second, after)


def gathered_dot(full, weight):
    depth = full.shape[2]
    return sum(dot(full[j], weight[j * depth : (j + 1) * depth, :]) for j in range(full.shape[0]))


def halves_dot(core, full, mine, other, section):
    half, depth = full.shape[0] // 2, full.shape[2]
    total = 0
    for owner, held in ((core, mine), (1 - core, other)):
        for j in range(half):
            total += dot(full[owner * half + j], held[pl.ds((section * half + j) * depth, depth), :])
    return total


def mesh_one_kernel(core_ref, full, mesh, w_out, mine, other, base, mesh_one, projected, later):
    core, width = core_ref[0], mesh.shape[1]
    mesh_one[...] = (mesh[...].astype(jnp.float32) + gathered_dot(full, w_out)).astype(mesh_one.dtype)
    projected[...] = (base[:, :width] + halves_dot(core, full, mine, other, 0)).astype(projected.dtype)
    later[...] = base[:, width:] + halves_dot(core, full, mine, other, 1)


def mesh_next_kernel(core_ref, full, mesh_one, w_out, mine, other, later, mesh_next, projected):
    mesh_next[...] = (mesh_one[...].astype(jnp.float32) + gathered_dot(full, w_out)).astype(mesh_next.dtype)
    projected[...] = (later[...] + halves_dot(core_ref[0], full, mine, other, 2)).astype(projected.dtype)


def mesh_step(kernel, like, kinds, core, *operands):
    return pl.pallas_call(
        kernel,
        out_shape=[jax.ShapeDtypeStruct(like.shape, kind) for kind in kinds],
        in_specs=[SMEM] + [VMEM] * len(operands),
        out_specs=[VMEM] * len(kinds),
        compiler_params=pltpu.CompilerParams(vmem_limit_bytes=10 << 20),
        cost_estimate=pl.CostEstimate(flops=len(kinds) << 27, bytes_accessed=1 << 22, transcendentals=0),
        name="mesh_step",
    )(core, *operands)


def window_of_exchanges(projected, later):
    below = shift(projected, 2)
    above = shift(projected, -2)
    other = exchange(projected, "region", lambda i: i ^ 1)
    other, later = lax.optimization_barrier((other, later))
    sent = [exchange(later, "chan", lambda i: i ^ 1), exchange(later, "chan", lambda i: 3 - i)]
    first = lax.axis_index("region") % 2 == 0
    half = projected.shape[0] // 2
    chosen = [jnp.where(first, above[rows], below[rows]) for rows in (slice(0, half), slice(half, None))]
    return [projected, below, above, other] + [core_pair(rows) for rows in chosen], sent


def window_of_pairs(projected):
    below = shift(projected, 2)
    above = shift(projected, -2)
    own = core_pair(projected)
    first = lax.axis_index("region") % 2 == 0
    outer = core_pair(jnp.where(first, above, below))
    last = jnp.where(first, below, above)
    return [outer, own, last]


def place_in_exchanged(index, rows, me):
    core = me & 1
    apart, row = index // rows - me, index % rows
    block = jnp.where(apart == 0, 0, jnp.where(apart == -2, 1, jnp.where(apart == 2, 2, 3)))
    half = rows // 2
    moved = 4 * rows + jnp.where(row < half, row, row + half) + (1 - core) * half
    near = (apart == 0) | (apart == 1 - 2 * core) | (apart == 2) | (apart == -2)
    return jnp.where(near, block * rows + row, moved)


def place_in_pairs(index, rows, me):
    shift_by = rows.bit_length() - 1
    apart = (index >> shift_by) - (me - (me & 1))
    block = jnp.where(apart == 2, 0, jnp.where(apart == -1, 1, jnp.where(apart == 0, 2, jnp.where(apart == 1, 3, 4))))
    return (block << shift_by) + (index & (rows - 1))


def scaled(weight, count):
    live = lax.broadcasted_iota(jnp.int32, weight.shape, 0) < count
    return jnp.where(live, weight, 0.0) / count.astype(jnp.float32)


def upright(v):
    if v.shape[0] < TILE:
        v = jnp.concatenate([v, jnp.zeros((TILE - v.shape[0], v.shape[1]), v.dtype)], axis=0)
    return v.T


def by_rows_kernel(slots, rows, group, sizes, index_ref, slot_ref, count_ref, receiver_ref, *refs):
    parts, out_ref = refs[: len(sizes)], refs[len(sizes)]
    window, receiver, fetched, total, weight_ref = refs[len(sizes) + 1 :]
    tall = upright(scaled(slot_ref[...], count_ref[...]))
    for s in range(2):
        weight_ref[pl.ds(s, rows, 2), :] = tall
    first = 0
    for part, size in zip(parts, sizes):
        half = part[...].astype(jnp.float32) * 0.5
        for s in range(2):
            window[pl.ds(2 * first + s, size, 2), :] = half[:, s * LANES : (s + 1) * LANES]
        first += size
    half = receiver_ref[...].astype(jnp.float32) * 0.5
    for s in range(2):
        receiver[pl.ds(s, rows, 2), :] = half[:, s * LANES : (s + 1) * LANES]

    def fetch(start, side):
        for u in range(group):
            for k in range(slots):
                at = ((u // 4) * slots + k) * TILE + (u % 4) * 2
                fetched[side, at : at + 2, :] = window[pl.ds(index_ref[k, start + u], 2), :]

    def add_up(start, side):
        for t in range(group // 4):
            row = pl.multiple_of(2 * start + TILE * t, TILE)
            mine = receiver[pl.ds(row, TILE), :]
            weight = weight_ref[pl.ds(row, TILE), :]
            acc = jnp.zeros((TILE, LANES), jnp.float32)
            for k in range(slots):
                at = (t * slots + k) * TILE
                h = fetched[side, at : at + TILE, :] + mine
                acc = acc + (h + h * jnp.tanh(h)) * weight[:, k : k + 1]
            total[pl.ds(row, TILE), :] = acc

    fetch(0, 0)

    def two_groups(j, carry):
        start = j * 2 * group
        fetch(start + group, 1)
        add_up(start, 0)
        fetch(jnp.minimum(start + 2 * group, rows - group), 0)
        add_up(start + group, 1)
        return carry

    lax.fori_loop(0, rows // (2 * group), two_groups, 0)
    for s in range(2):
        value = total[pl.ds(s, rows, 2), :].astype(out_ref.dtype)
        for j in range(out_ref.shape[0]):
            out_ref[j, :, s * LANES : (s + 1) * LANES] = value


def aggregate_by_rows(index, weights, counts, receivers, parts, copies, group=8):
    slots, rows = index.shape
    width = receivers.shape[1]
    sizes = tuple(part.shape[0] for part in parts)
    return pl.pallas_call(
        functools.partial(by_rows_kernel, slots, rows, group, sizes),
        out_shape=jax.ShapeDtypeStruct((copies, rows, width), receivers.dtype),
        in_specs=[SMEM] + [VMEM] * (3 + len(parts)),
        out_specs=VMEM,
        scratch_shapes=[
            pltpu.VMEM((2 * sum(sizes), LANES), jnp.float32),
            pltpu.VMEM((2 * rows, LANES), jnp.float32),
            pltpu.VMEM((2, group // 4 * slots * TILE, LANES), jnp.float32),
            pltpu.VMEM((2 * rows, LANES), jnp.float32),
            pltpu.VMEM((2 * rows, slots), jnp.float32),
        ],
        compiler_params=pltpu.CompilerParams(vmem_limit_bytes=14 << 20),
        cost_estimate=pl.CostEstimate(flops=1, bytes_accessed=1, transcendentals=0),
        name="aggregate_by_rows",
    )(index, weights, counts[None, :], receivers, *parts)


def by_matmul_kernel(slots, rows, block, sizes, me_ref, sender_ref, slot_ref, count_ref, receiver_ref, *refs):
    parts, out_ref = refs[: len(sizes)], refs[len(sizes)]
    window, index_ref, weight_ref = refs[len(sizes) + 1 :]
    index_ref[...] = upright(place_in_pairs(sender_ref[...], sum(sizes) // 5, me_ref[0]))
    weight_ref[...] = upright(scaled(slot_ref[...], count_ref[...]))
    first = 0
    for part, size in zip(parts, sizes):
        window[first : first + size, :] = part[...]
        first += size
    columns = lax.broadcasted_iota(jnp.int32, (block, first), 1).astype(jnp.int16)
    one, zero = jnp.bfloat16(1), jnp.bfloat16(0)

    def one_block(b, carry):
        at = pl.ds(pl.multiple_of(b * block, block), block)
        mine = receiver_ref[at, :].astype(jnp.float32)
        index, weight = index_ref[at, :], weight_ref[at, :]
        acc = jnp.zeros(mine.shape, jnp.float32)
        for k in range(slots):
            wanted = jnp.broadcast_to(index[:, k : k + 1], (block, LANES)).astype(jnp.int16)
            pick = [jnp.where(columns[:, j : j + LANES] == wanted, one, zero) for j in range(0, first, LANES)]
            fetched = dot(jnp.concatenate(pick, axis=1), window[...])
            h = (fetched + mine) * 0.5
            acc = acc + (h + h * jnp.tanh(h)) * weight[:, k : k + 1]
        for j in range(out_ref.shape[0]):
            out_ref[j, at, :] = acc.astype(out_ref.dtype)
        return carry

    lax.fori_loop(0, rows // block, one_block, 0)


def aggregate_by_matmul(senders, weights, counts, receivers, parts, copies, block=256):
    slots, (rows, width) = senders.shape[0], receivers.shape
    me = lax.axis_index("region").astype(jnp.int32)[None]
    sizes = tuple(part.shape[0] for part in parts)
    return pl.pallas_call(
        functools.partial(by_matmul_kernel, slots, rows, block, sizes),
        out_shape=jax.ShapeDtypeStruct((copies, rows, width), receivers.dtype),
        in_specs=[SMEM] + [VMEM] * (4 + len(parts)),
        out_specs=VMEM,
        scratch_shapes=[
            pltpu.VMEM((sum(sizes), width), jnp.bfloat16),
            pltpu.VMEM((rows, max(slots, TILE)), jnp.int32),
            pltpu.VMEM((rows, max(slots, TILE)), jnp.float32),
        ],
        compiler_params=pltpu.CompilerParams(vmem_limit_bytes=14 << 20),
        cost_estimate=pl.CostEstimate(
            flops=2 * slots * rows * sum(sizes) * width,
            bytes_accessed=2 * width * (sum(sizes) + 2 * rows),
            transcendentals=slots * rows * width,
        ),
        name="aggregate_by_matmul",
    )(me, senders, weights, counts[None, :], receivers, *parts)


def shards(
    grid_state,
    mesh_state,
    enc_send,
    enc_out,
    proc_send,
    proc_out,
    dec_send,
    dec_out,
    g2m_index,
    g2m_weight,
    g2m_count,
    m2m_index,
    m2m_weight,
    m2m_count,
    m2g_index,
    m2g_weight,
    m2g_count,
):
    n_grid, n_mesh = grid_state.shape[0], mesh_state.shape[0]
    bf16, f32 = jnp.bfloat16, jnp.float32
    core = lax.axis_index("region").astype(jnp.int32) % 2
    half = enc_out.shape[0] // 2
    own_rows = [lax.dynamic_slice_in_dim(w, core * half, half, axis=0) for w in (enc_out, proc_out)]
    packed = jnp.concatenate(own_rows + [mesh_state], axis=0)
    g2m = 2 * place_in_exchanged(g2m_index, n_grid, lax.axis_index("region").astype(jnp.int32))

    projected, far = project_by_exchanges(grid_state, enc_send, later=packed)
    window, nearer = window_of_exchanges(projected, packed)
    n = lax.axis_size("chan")
    agg = aggregate_by_rows(g2m, g2m_weight, g2m_count, mesh_state, window, 1)

    full = lax.all_gather(agg[0], "chan", axis=0)
    mine, base = combine([packed, *nearer, far], proc_send, dec_send, n_mesh, full)
    other = exchange(mine, "region", lambda i: i ^ 1)
    mesh_one, projected, later = mesh_step(
        mesh_one_kernel, mesh_state, (bf16, bf16, f32), core[None], full, mesh_state, enc_out, mine, other, base
    )
    agg = aggregate_by_matmul(m2m_index, m2m_weight, m2m_count, mesh_one, window_of_pairs(projected), n)
    mesh_next, projected = mesh_step(
        mesh_next_kernel, mesh_state, (bf16, bf16), core[None], gather_chan(agg), mesh_one, proc_out, mine, other, later
    )
    agg = aggregate_by_matmul(m2g_index, m2g_weight, m2g_count, grid_state, window_of_pairs(projected), 1)[0]
    grid_next, _ = project_by_exchanges(agg, dec_out, base=(grid_state,))
    return grid_next, mesh_next


def solution(mesh):
    by_both, by_chan = P("region", "chan"), P(None, "chan")
    edge = (P(None, "region"), P(None, "region"), P("region"))
    return jax.shard_map(
        shards,
        mesh=mesh,
        in_specs=(by_both,) * 2 + (by_chan,) * 6 + edge * 3,
        out_specs=(by_both, by_both),
        check_vma=False,
    )
```

```python
import functools

import jax
import jax.numpy as jnp
from jax import lax
from jax.experimental import pallas as pl
from jax.experimental.pallas import tpu as pltpu
from jax.sharding import PartitionSpec as P

LANES = 128
TILE = 8
VMEM = pl.BlockSpec(memory_space=pltpu.VMEM)
HBM = pl.BlockSpec(memory_space=pltpu.HBM)
SMEM = pl.BlockSpec(memory_space=pltpu.SMEM)


def exchange(shard, axis, partner):
    n = lax.axis_size(axis)
    return lax.ppermute(shard, axis, [(i, partner(i)) for i in range(n)])


def shift(shard, by):
    n = lax.axis_size("region")
    return lax.ppermute(shard, "region", [(i, i + by) for i in range(n) if 0 <= i + by < n])


def core_pair(shard):
    n = lax.axis_size("region")
    groups = [[i, i + 1] for i in range(0, n, 2)]
    return lax.all_gather(shard, "region", axis=0, tiled=True, axis_index_groups=groups)


def gather_chan(copies):
    return lax.all_to_all(copies, "chan", split_axis=0, concat_axis=0, tiled=True)


def dot(a, b):
    return jnp.dot(a, b, preferred_element_type=jnp.float32)


def partial_kernel(me_ref, own, near_top, near_low, other_top, other_low, weight, total):
    me = me_ref[0]
    rows, width = own.shape
    half = rows // 2

    def block_of(source):
        return weight[pl.ds(pl.multiple_of(source * width, width), width), :]

    mine, near, other = block_of(me), block_of(me ^ 1), block_of(3 - me)
    for first, from_near, from_other in ((0, near_top, other_top), (half, near_low, other_low)):
        at = slice(first, first + half)
        total[at, :] = dot(own[at, :], mine) + dot(from_near[...], near) + dot(from_other[...], other)


def last_kernel(me_ref, total, far_top, far_low, weight, *refs):
    base, out = refs[:-1], refs[-1]
    rows, width = total.shape
    half = rows // 2
    block = weight[pl.ds(pl.multiple_of((me_ref[0] ^ 2) * width, width), width), :]
    for first, far in ((0, far_top), (half, far_low)):
        at = slice(first, first + half)
        value = total[at, :] + dot(far[...], block)
        for ref in base:
            value = value + ref[at, :].astype(jnp.float32)
        out[at, :] = value.astype(out.dtype)


def project_by_exchanges(values, weight, base=(), later=None):
    assert lax.axis_size("chan") == 4
    me = lax.axis_index("chan").astype(jnp.int32)[None]
    rows, width = values.shape
    half = rows // 2
    near = functools.partial(exchange, axis="chan", partner=lambda i: i ^ 1)
    other = functools.partial(exchange, axis="chan", partner=lambda i: 3 - i)
    top, low = values[:half], values[half:]
    other_top, near_low = other(top), near(low)
    other_low, near_top = other(low), near(top)
    far_top, far_low = near(other_top), other(near_low)
    params = pltpu.CompilerParams(vmem_limit_bytes=10 << 20)
    total = pl.pallas_call(
        partial_kernel,
        out_shape=jax.ShapeDtypeStruct((rows, width), jnp.float32),
        in_specs=[SMEM] + [VMEM] * 6,
        out_specs=VMEM,
        compiler_params=params,
        cost_estimate=pl.CostEstimate(flops=6 * rows * width * width, bytes_accessed=10 * rows * width, transcendentals=0),
        name="first_blocks",
    )(me, values, near_top, near_low, other_top, other_low, weight)
    if later is not None:
        total, later = lax.optimization_barrier((total, later))
        later = exchange(later, "chan", lambda i: i ^ 2)
    out = pl.pallas_call(
        last_kernel,
        out_shape=jax.ShapeDtypeStruct((rows, width), values.dtype),
        in_specs=[SMEM] + [VMEM] * (4 + len(base)),
        out_specs=VMEM,
        compiler_params=params,
        cost_estimate=pl.CostEstimate(flops=2 * rows * width * width, bytes_accessed=10 * rows * width, transcendentals=0),
        name="last_block",
    )(me, total, far_top, far_low, weight, *base)
    return out, later


def combine_kernel(me_ref, own, near, other, far, first, second, _, mixed, base):
    me, width = me_ref[0], own.shape[1]
    rows, last = own.shape[0], base.shape[0]
    half = (rows - last) // 2
    blocks = [(me, own), (me ^ 1, near), (3 - me, other), (me ^ 2, far)]

    def product(start, size, weight):
        value = jnp.zeros((size, width), jnp.float32)
        for source, block in blocks:
            value += dot(block[pl.ds(start, size), :], weight[pl.ds(pl.multiple_of(source * width, width), width), :])
        return value

    for section, start, weight in ((0, 0, first), (1, 0, second), (2, half, second)):
        mixed[pl.ds(section * half, half), :] = product(start, half, weight).astype(mixed.dtype)
    base[:, :width] = product(2 * half, last, first)
    base[:, width:] = product(2 * half, last, second)


def combine(blocks, first, second, last, after):
    rows, width = blocks[0].shape
    return pl.pallas_call(
        combine_kernel,
        out_shape=(
            jax.ShapeDtypeStruct(((rows - last) // 2 * 3, width), blocks[0].dtype),
            jax.ShapeDtypeStruct((last, 2 * width), jnp.float32),
        ),
        in_specs=[SMEM] + [VMEM] * 6 + [HBM],
        out_specs=(VMEM, VMEM),
        compiler_params=pltpu.CompilerParams(vmem_limit_bytes=10 << 20),
        cost_estimate=pl.CostEstimate(flops=16 * rows * width * width, bytes_accessed=16 * rows * width, transcendentals=0),
        name="combine",
    )(lax.axis_index("chan").astype(jnp.int32)[None], *blocks, first, second, after)


def gathered_dot(full, weight):
    depth = full.shape[2]
    return sum(dot(full[j], weight[j * depth : (j + 1) * depth, :]) for j in range(full.shape[0]))


def halves_dot(core, full, mine, other, section):
    half, depth = full.shape[0] // 2, full.shape[2]
    total = 0
    for owner, held in ((core, mine), (1 - core, other)):
        for j in range(half):
            total += dot(full[owner * half + j], held[pl.ds((section * half + j) * depth, depth), :])
    return total


def mesh_one_kernel(core_ref, full, mesh, w_out, mine, other, base, mesh_one, projected, later):
    core, width = core_ref[0], mesh.shape[1]
    mesh_one[...] = (mesh[...].astype(jnp.float32) + gathered_dot(full, w_out)).astype(mesh_one.dtype)
    projected[...] = (base[:, :width] + halves_dot(core, full, mine, other, 0)).astype(projected.dtype)
    later[...] = base[:, width:] + halves_dot(core, full, mine, other, 1)


def mesh_next_kernel(core_ref, full, mesh_one, w_out, mine, other, later, mesh_next, projected):
    mesh_next[...] = (mesh_one[...].astype(jnp.float32) + gathered_dot(full, w_out)).astype(mesh_next.dtype)
    projected[...] = (later[...] + halves_dot(core_ref[0], full, mine, other, 2)).astype(projected.dtype)


def mesh_step(kernel, like, kinds, core, *operands):
    return pl.pallas_call(
        kernel,
        out_shape=[jax.ShapeDtypeStruct(like.shape, kind) for kind in kinds],
        in_specs=[SMEM] + [VMEM] * len(operands),
        out_specs=[VMEM] * len(kinds),
        compiler_params=pltpu.CompilerParams(vmem_limit_bytes=10 << 20),
        cost_estimate=pl.CostEstimate(flops=len(kinds) << 27, bytes_accessed=1 << 22, transcendentals=0),
        name="mesh_step",
    )(core, *operands)


def window_of_exchanges(projected, later):
    below = shift(projected, 2)
    above = shift(projected, -2)
    other = exchange(projected, "region", lambda i: i ^ 1)
    other, later = lax.optimization_barrier((other, later))
    sent = [exchange(later, "chan", lambda i: i ^ 1), exchange(later, "chan", lambda i: 3 - i)]
    first = lax.axis_index("region") % 2 == 0
    half = projected.shape[0] // 2
    chosen = [jnp.where(first, above[rows], below[rows]) for rows in (slice(0, half), slice(half, None))]
    return [projected, below, above, other] + [core_pair(rows) for rows in chosen], sent


def window_of_pairs(projected, fetch_own=None):
    below = shift(projected, 2)
    above = shift(projected, -2)
    own = core_pair(projected)
    if fetch_own is not None:
        above, own = lax.optimization_barrier((above, fetch_own(own)))
    first = lax.axis_index("region") % 2 == 0
    outer = core_pair(jnp.where(first, above, below))
    last = jnp.where(first, below, above)
    return own, [outer, last]


def place_in_exchanged(index, rows, me):
    core = me & 1
    apart, row = index // rows - me, index % rows
    block = jnp.where(apart == 0, 0, jnp.where(apart == -2, 1, jnp.where(apart == 2, 2, 3)))
    half = rows // 2
    moved = 4 * rows + jnp.where(row < half, row, row + half) + (1 - core) * half
    near = (apart == 0) | (apart == 1 - 2 * core) | (apart == 2) | (apart == -2)
    return jnp.where(near, block * rows + row, moved)


def place_in_pairs(index, rows, me, own):
    shift_by = rows.bit_length() - 1
    apart = (index >> shift_by) - (me - (me & 1))
    inside = (apart == 0) | (apart == 1)
    if own:
        block = jnp.where(inside, apart, 2)
    else:
        block = jnp.where(inside, apart + 3, jnp.where(apart == 2, 0, jnp.where(apart == -1, 1, 2)))
    return (block << shift_by) + (index & (rows - 1))


def scaled(weight, count):
    live = lax.broadcasted_iota(jnp.int32, weight.shape, 0) < count
    return jnp.where(live, weight, 0.0) / count.astype(jnp.float32)


def upright(v):
    if v.shape[0] < TILE:
        v = jnp.concatenate([v, jnp.zeros((TILE - v.shape[0], v.shape[1]), v.dtype)], axis=0)
    return v.T


def by_rows_kernel(slots, rows, group, sizes, index_ref, slot_ref, count_ref, receiver_ref, *refs):
    parts, out_ref = refs[: len(sizes)], refs[len(sizes)]
    window, receiver, fetched, total, weight_ref = refs[len(sizes) + 1 :]
    tall = upright(scaled(slot_ref[...], count_ref[...]))
    for s in range(2):
        weight_ref[pl.ds(s, rows, 2), :] = tall
    first = 0
    for part, size in zip(parts, sizes):
        half = part[...].astype(jnp.float32) * 0.5
        for s in range(2):
            window[pl.ds(2 * first + s, size, 2), :] = half[:, s * LANES : (s + 1) * LANES]
        first += size
    half = receiver_ref[...].astype(jnp.float32) * 0.5
    for s in range(2):
        receiver[pl.ds(s, rows, 2), :] = half[:, s * LANES : (s + 1) * LANES]

    def fetch(start, side):
        for u in range(group):
            for k in range(slots):
                at = ((u // 4) * slots + k) * TILE + (u % 4) * 2
                fetched[side, at : at + 2, :] = window[pl.ds(index_ref[k, start + u], 2), :]

    def add_up(start, side):
        for t in range(group // 4):
            row = pl.multiple_of(2 * start + TILE * t, TILE)
            mine = receiver[pl.ds(row, TILE), :]
            weight = weight_ref[pl.ds(row, TILE), :]
            acc = jnp.zeros((TILE, LANES), jnp.float32)
            for k in range(slots):
                at = (t * slots + k) * TILE
                h = fetched[side, at : at + TILE, :] + mine
                acc = acc + (h + h * jnp.tanh(h)) * weight[:, k : k + 1]
            total[pl.ds(row, TILE), :] = acc

    fetch(0, 0)

    def two_groups(j, carry):
        start = j * 2 * group
        fetch(start + group, 1)
        add_up(start, 0)
        fetch(jnp.minimum(start + 2 * group, rows - group), 0)
        add_up(start + group, 1)
        return carry

    lax.fori_loop(0, rows // (2 * group), two_groups, 0)
    for s in range(2):
        value = total[pl.ds(s, rows, 2), :].astype(out_ref.dtype)
        for j in range(out_ref.shape[0]):
            out_ref[j, :, s * LANES : (s + 1) * LANES] = value


def aggregate_by_rows(index, weights, counts, receivers, parts, copies, group=8):
    slots, rows = index.shape
    width = receivers.shape[1]
    sizes = tuple(part.shape[0] for part in parts)
    return pl.pallas_call(
        functools.partial(by_rows_kernel, slots, rows, group, sizes),
        out_shape=jax.ShapeDtypeStruct((copies, rows, width), receivers.dtype),
        in_specs=[SMEM] + [VMEM] * (3 + len(parts)),
        out_specs=VMEM,
        scratch_shapes=[
            pltpu.VMEM((2 * sum(sizes), LANES), jnp.float32),
            pltpu.VMEM((2 * rows, LANES), jnp.float32),
            pltpu.VMEM((2, group // 4 * slots * TILE, LANES), jnp.float32),
            pltpu.VMEM((2 * rows, LANES), jnp.float32),
            pltpu.VMEM((2 * rows, slots), jnp.float32),
        ],
        compiler_params=pltpu.CompilerParams(vmem_limit_bytes=14 << 20),
        cost_estimate=pl.CostEstimate(flops=1, bytes_accessed=1, transcendentals=0),
        name="aggregate_by_rows",
    )(index, weights, counts[None, :], receivers, *parts)


def pick_rows(index, columns, window):
    wanted = jnp.broadcast_to(index, (index.shape[0], LANES)).astype(jnp.int16)
    one, zero = jnp.bfloat16(1), jnp.bfloat16(0)
    picks = [jnp.where(columns[:, j : j + LANES] == wanted, one, zero) for j in range(0, columns.shape[1], LANES)]
    return dot(jnp.concatenate(picks, axis=1), window[...])


def fetch_kernel(slots, block, me_ref, sender_ref, window, out_ref, index_ref):
    depth, rows = window.shape[0], sender_ref.shape[1]
    index_ref[...] = upright(place_in_pairs(sender_ref[...], depth // 2, me_ref[0], True))
    columns = lax.broadcasted_iota(jnp.int32, (block, depth), 1).astype(jnp.int16)

    def one_block(b, carry):
        at = pl.ds(pl.multiple_of(b * block, block), block)
        index = index_ref[at, :]
        for k in range(slots):
            out_ref[k, at, :] = pick_rows(index[:, k : k + 1], columns, window).astype(out_ref.dtype)
        return carry

    lax.fori_loop(0, rows // block, one_block, 0)


def fetch_own(senders, window, block=256):
    slots, rows = senders.shape
    width = window.shape[1]
    me = lax.axis_index("region").astype(jnp.int32)[None]
    return pl.pallas_call(
        functools.partial(fetch_kernel, slots, block),
        out_shape=jax.ShapeDtypeStruct((slots, rows, width), window.dtype),
        in_specs=[SMEM, VMEM, VMEM],
        out_specs=VMEM,
        scratch_shapes=[pltpu.VMEM((rows, max(slots, TILE)), jnp.int32)],
        compiler_params=pltpu.CompilerParams(vmem_limit_bytes=10 << 20),
        cost_estimate=pl.CostEstimate(
            flops=2 * slots * rows * window.shape[0] * width, bytes_accessed=2 * slots * rows * width, transcendentals=0
        ),
        name="fetch_own",
    )(me, senders, window)


def by_matmul_kernel(slots, block, sizes, ahead, me_ref, sender_ref, slot_ref, count_ref, receiver_ref, *refs):
    fetched_ref, refs = (refs[0], refs[1:]) if ahead else (None, refs)
    parts, out_ref = refs[: len(sizes)], refs[len(sizes)]
    window, index_ref, weight_ref = refs[len(sizes) + 1 :]
    depth, rows = sum(sizes), sender_ref.shape[1]
    index_ref[...] = upright(place_in_pairs(sender_ref[...], depth // (3 if ahead else 5), me_ref[0], False))
    weight_ref[...] = upright(scaled(slot_ref[...], count_ref[...]))
    first = 0
    for part, size in zip(parts, sizes):
        window[first : first + size, :] = part[...]
        first += size
    columns = lax.broadcasted_iota(jnp.int32, (block, depth), 1).astype(jnp.int16)

    def one_block(b, carry):
        at = pl.ds(pl.multiple_of(b * block, block), block)
        mine = receiver_ref[at, :].astype(jnp.float32)
        index, weight = index_ref[at, :], weight_ref[at, :]
        acc = jnp.zeros(mine.shape, jnp.float32)
        for k in range(slots):
            fetched = pick_rows(index[:, k : k + 1], columns, window)
            if ahead:
                fetched += fetched_ref[k, at, :].astype(jnp.float32)
            h = (fetched + mine) * 0.5
            acc = acc + (h + h * jnp.tanh(h)) * weight[:, k : k + 1]
        for j in range(out_ref.shape[0]):
            out_ref[j, at, :] = acc.astype(out_ref.dtype)
        return carry

    lax.fori_loop(0, rows // block, one_block, 0)


def aggregate_by_matmul(senders, weights, counts, receivers, projected, copies, ahead, block=256):
    slots, (rows, width) = senders.shape[0], receivers.shape
    me = lax.axis_index("region").astype(jnp.int32)[None]
    own, parts = window_of_pairs(projected, functools.partial(fetch_own, senders) if ahead else None)
    before, parts = ([own], parts) if ahead else ([], parts + [own])
    sizes = tuple(part.shape[0] for part in parts)
    return pl.pallas_call(
        functools.partial(by_matmul_kernel, slots, block, sizes, ahead),
        out_shape=jax.ShapeDtypeStruct((copies, rows, width), receivers.dtype),
        in_specs=[SMEM] + [VMEM] * (4 + len(before) + len(parts)),
        out_specs=VMEM,
        scratch_shapes=[
            pltpu.VMEM((sum(sizes), width), jnp.bfloat16),
            pltpu.VMEM((rows, max(slots, TILE)), jnp.int32),
            pltpu.VMEM((rows, max(slots, TILE)), jnp.float32),
        ],
        compiler_params=pltpu.CompilerParams(vmem_limit_bytes=14 << 20),
        cost_estimate=pl.CostEstimate(
            flops=2 * slots * rows * sum(sizes) * width,
            bytes_accessed=2 * width * (sum(sizes) + 2 * rows),
            transcendentals=slots * rows * width,
        ),
        name="aggregate_by_matmul",
    )(me, senders, weights, counts[None, :], receivers, *before, *parts)


def shards(
    grid_state,
    mesh_state,
    enc_send,
    enc_out,
    proc_send,
    proc_out,
    dec_send,
    dec_out,
    g2m_index,
    g2m_weight,
    g2m_count,
    m2m_index,
    m2m_weight,
    m2m_count,
    m2g_index,
    m2g_weight,
    m2g_count,
):
    n_grid, n_mesh = grid_state.shape[0], mesh_state.shape[0]
    bf16, f32 = jnp.bfloat16, jnp.float32
    core = lax.axis_index("region").astype(jnp.int32) % 2
    half = enc_out.shape[0] // 2
    own_rows = [lax.dynamic_slice_in_dim(w, core * half, half, axis=0) for w in (enc_out, proc_out)]
    packed = jnp.concatenate(own_rows + [mesh_state], axis=0)
    g2m = 2 * place_in_exchanged(g2m_index, n_grid, lax.axis_index("region").astype(jnp.int32))

    projected, far = project_by_exchanges(grid_state, enc_send, later=packed)
    window, nearer = window_of_exchanges(projected, packed)
    n = lax.axis_size("chan")
    agg = aggregate_by_rows(g2m, g2m_weight, g2m_count, mesh_state, window, 1)

    full = lax.all_gather(agg[0], "chan", axis=0)
    mine, base = combine([packed, *nearer, far], proc_send, dec_send, n_mesh, full)
    other = exchange(mine, "region", lambda i: i ^ 1)
    mesh_one, projected, later = mesh_step(
        mesh_one_kernel, mesh_state, (bf16, bf16, f32), core[None], full, mesh_state, enc_out, mine, other, base
    )
    agg = aggregate_by_matmul(m2m_index, m2m_weight, m2m_count, mesh_one, projected, n, True)
    mesh_next, projected = mesh_step(
        mesh_next_kernel, mesh_state, (bf16, bf16), core[None], gather_chan(agg), mesh_one, proc_out, mine, other, later
    )
    agg = aggregate_by_matmul(m2g_index, m2g_weight, m2g_count, grid_state, projected, 1, False)[0]
    grid_next, _ = project_by_exchanges(agg, dec_out, base=(grid_state,))
    return grid_next, mesh_next


def solution(mesh):
    by_both, by_chan = P("region", "chan"), P(None, "chan")
    edge = (P(None, "region"), P(None, "region"), P("region"))
    return jax.shard_map(
        shards,
        mesh=mesh,
        in_specs=(by_both,) * 2 + (by_chan,) * 6 + edge * 3,
        out_specs=(by_both, by_both),
        check_vma=False,
    )
```

```python
import functools

import jax
import jax.numpy as jnp
from jax import lax
from jax.experimental import pallas as pl
from jax.experimental.pallas import tpu as pltpu
from jax.sharding import PartitionSpec as P

LANES = 128
TILE = 8
VMEM = pl.BlockSpec(memory_space=pltpu.VMEM)
HBM = pl.BlockSpec(memory_space=pltpu.HBM)
SMEM = pl.BlockSpec(memory_space=pltpu.SMEM)


def exchange(shard, axis, partner):
    n = lax.axis_size(axis)
    return lax.ppermute(shard, axis, [(i, partner(i)) for i in range(n)])


def shift(shard, by):
    n = lax.axis_size("region")
    return lax.ppermute(shard, "region", [(i, i + by) for i in range(n) if 0 <= i + by < n])


def core_pair(shard):
    n = lax.axis_size("region")
    groups = [[i, i + 1] for i in range(0, n, 2)]
    return lax.all_gather(shard, "region", axis=0, tiled=True, axis_index_groups=groups)


def gather_chan(copies):
    return lax.all_to_all(copies, "chan", split_axis=0, concat_axis=0, tiled=True)


def dot(a, b):
    return jnp.dot(a, b, preferred_element_type=jnp.float32)


def partial_kernel(me_ref, own, near_top, near_low, other_top, other_low, weight, total):
    me = me_ref[0]
    rows, width = own.shape
    half = rows // 2

    def block_of(source):
        return weight[pl.ds(pl.multiple_of(source * width, width), width), :]

    mine, near, other = block_of(me), block_of(me ^ 1), block_of(3 - me)
    for first, from_near, from_other in ((0, near_top, other_top), (half, near_low, other_low)):
        at = slice(first, first + half)
        total[at, :] = dot(own[at, :], mine) + dot(from_near[...], near) + dot(from_other[...], other)


def last_kernel(me_ref, total, far_top, far_low, weight, *refs):
    base, out = refs[:-1], refs[-1]
    rows, width = total.shape
    half = rows // 2
    block = weight[pl.ds(pl.multiple_of((me_ref[0] ^ 2) * width, width), width), :]
    for first, far in ((0, far_top), (half, far_low)):
        at = slice(first, first + half)
        value = total[at, :] + dot(far[...], block)
        for ref in base:
            value = value + ref[at, :].astype(jnp.float32)
        out[at, :] = value.astype(out.dtype)


def project_by_exchanges(values, weight, base=(), later=None):
    assert lax.axis_size("chan") == 4
    me = lax.axis_index("chan").astype(jnp.int32)[None]
    rows, width = values.shape
    half = rows // 2
    near = functools.partial(exchange, axis="chan", partner=lambda i: i ^ 1)
    other = functools.partial(exchange, axis="chan", partner=lambda i: 3 - i)
    top, low = values[:half], values[half:]
    other_top, near_low = other(top), near(low)
    other_low, near_top = other(low), near(top)
    far_top, far_low = near(other_top), other(near_low)
    params = pltpu.CompilerParams(vmem_limit_bytes=10 << 20)
    total = pl.pallas_call(
        partial_kernel,
        out_shape=jax.ShapeDtypeStruct((rows, width), jnp.float32),
        in_specs=[SMEM] + [VMEM] * 6,
        out_specs=VMEM,
        compiler_params=params,
        cost_estimate=pl.CostEstimate(flops=6 * rows * width * width, bytes_accessed=10 * rows * width, transcendentals=0),
        name="first_blocks",
    )(me, values, near_top, near_low, other_top, other_low, weight)
    if later is not None:
        total, later = lax.optimization_barrier((total, later))
        later = exchange(later, "chan", lambda i: i ^ 2)
    out = pl.pallas_call(
        last_kernel,
        out_shape=jax.ShapeDtypeStruct((rows, width), values.dtype),
        in_specs=[SMEM] + [VMEM] * (4 + len(base)),
        out_specs=VMEM,
        compiler_params=params,
        cost_estimate=pl.CostEstimate(flops=2 * rows * width * width, bytes_accessed=10 * rows * width, transcendentals=0),
        name="last_block",
    )(me, total, far_top, far_low, weight, *base)
    return out, later


def combine_kernel(me_ref, own, near, other, far, first, second, _, mixed, base):
    me, width = me_ref[0], own.shape[1]
    rows, last = own.shape[0], base.shape[0]
    half = (rows - last) // 2
    blocks = [(me, own), (me ^ 1, near), (3 - me, other), (me ^ 2, far)]

    def product(start, size, weight):
        value = jnp.zeros((size, width), jnp.float32)
        for source, block in blocks:
            value += dot(block[pl.ds(start, size), :], weight[pl.ds(pl.multiple_of(source * width, width), width), :])
        return value

    for section, start, weight in ((0, 0, first), (1, 0, second), (2, half, second)):
        mixed[pl.ds(section * half, half), :] = product(start, half, weight).astype(mixed.dtype)
    base[:, :width] = product(2 * half, last, first)
    base[:, width:] = product(2 * half, last, second)


def combine(blocks, first, second, last, after):
    rows, width = blocks[0].shape
    return pl.pallas_call(
        combine_kernel,
        out_shape=(
            jax.ShapeDtypeStruct(((rows - last) // 2 * 3, width), blocks[0].dtype),
            jax.ShapeDtypeStruct((last, 2 * width), jnp.float32),
        ),
        in_specs=[SMEM] + [VMEM] * 6 + [HBM],
        out_specs=(VMEM, VMEM),
        compiler_params=pltpu.CompilerParams(vmem_limit_bytes=10 << 20),
        cost_estimate=pl.CostEstimate(flops=16 * rows * width * width, bytes_accessed=16 * rows * width, transcendentals=0),
        name="combine",
    )(lax.axis_index("chan").astype(jnp.int32)[None], *blocks, first, second, after)


def gathered_dot(full, weight):
    depth = full.shape[2]
    return sum(dot(full[j], weight[j * depth : (j + 1) * depth, :]) for j in range(full.shape[0]))


def halves_dot(core, full, mine, other, section):
    half, depth = full.shape[0] // 2, full.shape[2]
    total = 0
    for owner, held in ((core, mine), (1 - core, other)):
        for j in range(half):
            total += dot(full[owner * half + j], held[pl.ds((section * half + j) * depth, depth), :])
    return total


def mesh_one_kernel(core_ref, full, mesh, w_out, mine, other, base, mesh_one, projected, later):
    core, width = core_ref[0], mesh.shape[1]
    mesh_one[...] = (mesh[...].astype(jnp.float32) + gathered_dot(full, w_out)).astype(mesh_one.dtype)
    projected[...] = (base[:, :width] + halves_dot(core, full, mine, other, 0)).astype(projected.dtype)
    later[...] = base[:, width:] + halves_dot(core, full, mine, other, 1)


def mesh_next_kernel(core_ref, full, mesh_one, w_out, mine, other, later, mesh_next, projected):
    mesh_next[...] = (mesh_one[...].astype(jnp.float32) + gathered_dot(full, w_out)).astype(mesh_next.dtype)
    projected[...] = (later[...] + halves_dot(core_ref[0], full, mine, other, 2)).astype(projected.dtype)


def mesh_step(kernel, like, kinds, core, *operands):
    return pl.pallas_call(
        kernel,
        out_shape=[jax.ShapeDtypeStruct(like.shape, kind) for kind in kinds],
        in_specs=[SMEM] + [VMEM] * len(operands),
        out_specs=[VMEM] * len(kinds),
        compiler_params=pltpu.CompilerParams(vmem_limit_bytes=10 << 20),
        cost_estimate=pl.CostEstimate(flops=len(kinds) << 27, bytes_accessed=1 << 22, transcendentals=0),
        name="mesh_step",
    )(core, *operands)


def window_of_exchanges(projected, later):
    below = shift(projected, 2)
    above = shift(projected, -2)
    other = exchange(projected, "region", lambda i: i ^ 1)
    other, later = lax.optimization_barrier((other, later))
    sent = [exchange(later, "chan", lambda i: i ^ 1), exchange(later, "chan", lambda i: 3 - i)]
    first = lax.axis_index("region") % 2 == 0
    half = projected.shape[0] // 2
    chosen = [jnp.where(first, above[rows], below[rows]) for rows in (slice(0, half), slice(half, None))]
    return [projected, below, above, other] + [core_pair(rows) for rows in chosen], sent


def window_of_pairs(projected):
    below = shift(projected, 2)
    above = shift(projected, -2)
    own = core_pair(projected)
    first = lax.axis_index("region") % 2 == 0
    outer = core_pair(jnp.where(first, above, below))
    last = jnp.where(first, below, above)
    return [outer, own, last]


def place_in_exchanged(index, rows, me):
    core = me & 1
    apart, row = index // rows - me, index % rows
    block = jnp.where(apart == 0, 0, jnp.where(apart == -2, 1, jnp.where(apart == 2, 2, 3)))
    half = rows // 2
    moved = 4 * rows + jnp.where(row < half, row, row + half) + (1 - core) * half
    near = (apart == 0) | (apart == 1 - 2 * core) | (apart == 2) | (apart == -2)
    return jnp.where(near, block * rows + row, moved)


def place_in_pairs(index, rows, me):
    shift_by = rows.bit_length() - 1
    apart = (index >> shift_by) - (me - (me & 1))
    block = jnp.where(apart == 2, 0, jnp.where(apart == -1, 1, jnp.where(apart == 0, 2, jnp.where(apart == 1, 3, 4))))
    return (block << shift_by) + (index & (rows - 1))


def scaled(weight, count):
    live = lax.broadcasted_iota(jnp.int32, weight.shape, 0) < count
    return jnp.where(live, weight, 0.0) / count.astype(jnp.float32)


def upright(v):
    if v.shape[0] < TILE:
        v = jnp.concatenate([v, jnp.zeros((TILE - v.shape[0], v.shape[1]), v.dtype)], axis=0)
    return v.T


def by_rows_kernel(slots, rows, group, sizes, index_ref, slot_ref, count_ref, receiver_ref, *refs):
    parts, out_ref = refs[: len(sizes)], refs[len(sizes)]
    window, receiver, fetched, total, weight_ref = refs[len(sizes) + 1 :]
    tall = upright(scaled(slot_ref[...], count_ref[...]))
    for s in range(2):
        weight_ref[pl.ds(s, rows, 2), :] = tall
    first = 0
    for part, size in zip(parts, sizes):
        half = part[...].astype(jnp.float32) * 0.5
        for s in range(2):
            window[pl.ds(2 * first + s, size, 2), :] = half[:, s * LANES : (s + 1) * LANES]
        first += size
    half = receiver_ref[...].astype(jnp.float32) * 0.5
    for s in range(2):
        receiver[pl.ds(s, rows, 2), :] = half[:, s * LANES : (s + 1) * LANES]

    def fetch(start, side):
        for u in range(group):
            for k in range(slots):
                at = ((u // 4) * slots + k) * TILE + (u % 4) * 2
                fetched[side, at : at + 2, :] = window[pl.ds(index_ref[k, start + u], 2), :]

    def add_up(start, side):
        for t in range(group // 4):
            row = pl.multiple_of(2 * start + TILE * t, TILE)
            mine = receiver[pl.ds(row, TILE), :]
            weight = weight_ref[pl.ds(row, TILE), :]
            acc = jnp.zeros((TILE, LANES), jnp.float32)
            for k in range(slots):
                at = (t * slots + k) * TILE
                h = fetched[side, at : at + TILE, :] + mine
                acc = acc + (h + h * jnp.tanh(h)) * weight[:, k : k + 1]
            total[pl.ds(row, TILE), :] = acc

    fetch(0, 0)

    def two_groups(j, carry):
        start = j * 2 * group
        fetch(start + group, 1)
        add_up(start, 0)
        fetch(jnp.minimum(start + 2 * group, rows - group), 0)
        add_up(start + group, 1)
        return carry

    lax.fori_loop(0, rows // (2 * group), two_groups, 0)
    for s in range(2):
        value = total[pl.ds(s, rows, 2), :].astype(out_ref.dtype)
        for j in range(out_ref.shape[0]):
            out_ref[j, :, s * LANES : (s + 1) * LANES] = value


def aggregate_by_rows(index, weights, counts, receivers, parts, copies, group=8):
    slots, rows = index.shape
    width = receivers.shape[1]
    sizes = tuple(part.shape[0] for part in parts)
    return pl.pallas_call(
        functools.partial(by_rows_kernel, slots, rows, group, sizes),
        out_shape=jax.ShapeDtypeStruct((copies, rows, width), receivers.dtype),
        in_specs=[SMEM] + [VMEM] * (3 + len(parts)),
        out_specs=VMEM,
        scratch_shapes=[
            pltpu.VMEM((2 * sum(sizes), LANES), jnp.float32),
            pltpu.VMEM((2 * rows, LANES), jnp.float32),
            pltpu.VMEM((2, group // 4 * slots * TILE, LANES), jnp.float32),
            pltpu.VMEM((2 * rows, LANES), jnp.float32),
            pltpu.VMEM((2 * rows, slots), jnp.float32),
        ],
        compiler_params=pltpu.CompilerParams(vmem_limit_bytes=14 << 20),
        cost_estimate=pl.CostEstimate(flops=1, bytes_accessed=1, transcendentals=0),
        name="aggregate_by_rows",
    )(index, weights, counts[None, :], receivers, *parts)


def by_matmul_kernel(slots, rows, block, sizes, me_ref, sender_ref, slot_ref, count_ref, receiver_ref, *refs):
    parts, out_ref = refs[: len(sizes)], refs[len(sizes)]
    window, index_ref, weight_ref = refs[len(sizes) + 1 :]
    index_ref[...] = upright(place_in_pairs(sender_ref[...], sum(sizes) // 5, me_ref[0]))
    weight_ref[...] = upright(scaled(slot_ref[...], count_ref[...]))
    first = 0
    for part, size in zip(parts, sizes):
        window[first : first + size, :] = part[...]
        first += size
    columns = lax.broadcasted_iota(jnp.int32, (block, first), 1).astype(jnp.int16)
    one, zero = jnp.bfloat16(1), jnp.bfloat16(0)

    def one_block(b, carry):
        at = pl.ds(pl.multiple_of(b * block, block), block)
        mine = receiver_ref[at, :].astype(jnp.float32)
        index, weight = index_ref[at, :], weight_ref[at, :]
        acc = jnp.zeros(mine.shape, jnp.float32)
        for k in range(slots):
            wanted = jnp.broadcast_to(index[:, k : k + 1], (block, LANES)).astype(jnp.int16)
            pick = [jnp.where(columns[:, j : j + LANES] == wanted, one, zero) for j in range(0, first, LANES)]
            fetched = dot(jnp.concatenate(pick, axis=1), window[...])
            h = (fetched + mine) * 0.5
            acc = acc + (h + h * jnp.tanh(h)) * weight[:, k : k + 1]
        for j in range(out_ref.shape[0]):
            out_ref[j, at, :] = acc.astype(out_ref.dtype)
        return carry

    lax.fori_loop(0, rows // block, one_block, 0)


def aggregate_by_matmul(senders, weights, counts, receivers, parts, copies, block=256):
    slots, (rows, width) = senders.shape[0], receivers.shape
    me = lax.axis_index("region").astype(jnp.int32)[None]
    sizes = tuple(part.shape[0] for part in parts)
    return pl.pallas_call(
        functools.partial(by_matmul_kernel, slots, rows, block, sizes),
        out_shape=jax.ShapeDtypeStruct((copies, rows, width), receivers.dtype),
        in_specs=[SMEM] + [VMEM] * (4 + len(parts)),
        out_specs=VMEM,
        scratch_shapes=[
            pltpu.VMEM((sum(sizes), width), jnp.bfloat16),
            pltpu.VMEM((rows, max(slots, TILE)), jnp.int32),
            pltpu.VMEM((rows, max(slots, TILE)), jnp.float32),
        ],
        compiler_params=pltpu.CompilerParams(vmem_limit_bytes=14 << 20),
        cost_estimate=pl.CostEstimate(
            flops=2 * slots * rows * sum(sizes) * width,
            bytes_accessed=2 * width * (sum(sizes) + 2 * rows),
            transcendentals=slots * rows * width,
        ),
        name="aggregate_by_matmul",
    )(me, senders, weights, counts[None, :], receivers, *parts)


def shards(
    grid_state,
    mesh_state,
    enc_send,
    enc_out,
    proc_send,
    proc_out,
    dec_send,
    dec_out,
    g2m_index,
    g2m_weight,
    g2m_count,
    m2m_index,
    m2m_weight,
    m2m_count,
    m2g_index,
    m2g_weight,
    m2g_count,
):
    n_grid, n_mesh = grid_state.shape[0], mesh_state.shape[0]
    bf16, f32 = jnp.bfloat16, jnp.float32
    core = lax.axis_index("region").astype(jnp.int32) % 2
    half = enc_out.shape[0] // 2
    own_rows = [lax.dynamic_slice_in_dim(w, core * half, half, axis=0) for w in (enc_out, proc_out)]
    packed = jnp.concatenate(own_rows + [mesh_state], axis=0)
    g2m = 2 * place_in_exchanged(g2m_index, n_grid, lax.axis_index("region").astype(jnp.int32))

    projected, far = project_by_exchanges(grid_state, enc_send, later=packed)
    window, nearer = window_of_exchanges(projected, packed)
    n = lax.axis_size("chan")
    agg = aggregate_by_rows(g2m, g2m_weight, g2m_count, mesh_state, window, 1)

    full = lax.all_gather(agg[0], "chan", axis=0)
    mine, base = combine([packed, *nearer, far], proc_send, dec_send, n_mesh, full)
    other = exchange(mine, "region", lambda i: i ^ 1)
    mesh_one, projected, later = mesh_step(
        mesh_one_kernel, mesh_state, (bf16, bf16, f32), core[None], full, mesh_state, enc_out, mine, other, base
    )
    agg = aggregate_by_matmul(m2m_index, m2m_weight, m2m_count, mesh_one, window_of_pairs(projected), n)
    mesh_next, projected = mesh_step(
        mesh_next_kernel, mesh_state, (bf16, bf16), core[None], gather_chan(agg), mesh_one, proc_out, mine, other, later
    )
    agg = aggregate_by_matmul(m2g_index, m2g_weight, m2g_count, grid_state, window_of_pairs(projected), 1, block=512)[0]
    grid_next, _ = project_by_exchanges(agg, dec_out, base=(grid_state,))
    return grid_next, mesh_next


def solution(mesh):
    by_both, by_chan = P("region", "chan"), P(None, "chan")
    edge = (P(None, "region"), P(None, "region"), P("region"))
    return jax.shard_map(
        shards,
        mesh=mesh,
        in_specs=(by_both,) * 2 + (by_chan,) * 6 + edge * 3,
        out_specs=(by_both, by_both),
        check_vma=False,
    )
```
